32 devices in a mesh: groups: 2 (over x), req: 8 (over z, y), tp: 2 (over core).
Axes of the slice: x: 2, y: 2, z: 4, core: 2. Of those that a mesh axis runs over, the one named last changes fastest.
Arguments:
- ssm_state: float32 [128, 16, 16384], P(('groups', 'req'), None, 'tp'), parts along dimension 0, may hold values from -6 to 6
- conv_state: float32 [128, 3, 16384], P(('groups', 'req'), None, 'tp'), parts along dimension 0, may hold values from -6 to 6
- token_input: bfloat16 [128, 2, 16384], P('groups', None, ('tp', 'req')), parts along dimension 0, may hold values from -6 to 6
- gate_input: bfloat16 [128, 2, 16384], P('groups', None, ('tp', 'req')), parts along dimension 0, may hold values from -6 to 6
- conv_weight: float32 [4, 16384], P(None, 'tp'), may hold values from -3 to 3
- conv_bias: float32 [16384], P('tp'), may hold values from -3 to 3
- proj_weight: bfloat16 [16384, 544], P(('tp', 'req')), may hold values from -0.046875 to 0.046875
- dt_weight: bfloat16 [512, 16384], P(None, ('tp', 'req')), may hold values from -0.25 to 0.25
- dt_bias: float32 [16384], P('tp'), may hold values from -3 to 0.5
- decay_log: float32 [16, 16384], P(None, 'tp'), may hold values from 0 to 2.7
- skip_gain: float32 [16384], P('tp'), may hold values from 0.5 to 1.5
- queries: bfloat16 [128, 2, 8192], P(('groups', 'req'), None, 'tp'), parts along dimension 0, may hold values from -6 to 6
- kv_pages: bfloat16 [2, 2048, 16, 1024], P(None, ('groups', 'req'), None, 'tp'), parts along dimension 1, may hold values from -6 to 6
- new_kv: bfloat16 [128, 2, 2, 1024], P(('groups', 'req'), None, None, 'tp'), parts along dimension 0, may hold values from -6 to 6
- page_table: int32 [16, 128], P(('groups', 'req')), parts along dimension 0, may hold values from 0 to 127, each once within a row
- context_len: int32 [128], P(('groups', 'req')), parts along dimension 0, may hold values from 1 to 256
- decode_row: int32 [128], P('groups'), parts along dimension 0, may hold values from 0 to 63, each once
Outputs:
- mamba_out: bfloat16 [128, 2, 16384], P('groups', None, ('tp', 'req')), parts along dimension 0
- attention_out: bfloat16 [128, 2, 8192], P('groups', None, ('tp', 'req')), parts along dimension 0
The draws below stay inside these ranges and needn't reach their ends.
There are 2 independent parts, one for each index of `groups`. The reference program is written for one: setup_inputs(seed, part) draws one part's arguments, and reference() takes and returns one part's arrays. A program takes and returns all parts, laid end to end along the dimension named above; an argument that names none is the same for every part. Nothing has to cross between parts.
Inputs may be any that keep to these rules, and one draw needn't show every extreme that they name: `page_table`: row d lists each of the 128 pages of pool d once; slot j of that pool owns entries j * 16 to (j + 1) * 16 - 1.
All inputs are finite; a program needn't handle non-finite values.
Results may differ from the reference program's by a relative error of at most 0.0057.
Values may be sent and summed in bfloat16 or wider, within the bound.
A program may use at most 128 MiB of HBM per device.

```python
import math
import jax
import jax.numpy as jnp
from jax import lax

DI = 16384
STATE = 16
CONV = 4
DT_RANK = 512
HQ = 64
KVH = 8
HD = 128
PAGE = 16
MAXP = 16
STEPS = 2
REQ_DEV = 8
R = 64
PAGES_DEV = 128
PAGES = 1024
MAXLEN = 256
XW = 544
N_REQ = 8


def draw_queries(key, part):
    key = jax.random.fold_in(key, 11)
    first = jax.random.fold_in(key, 0)
    noise = jax.random.normal(first, (R, STEPS, HQ, HD), jnp.float32)
    values = noise
    return jnp.clip(values, -6.0, 6.0).reshape(R, STEPS, HQ * HD).astype(jnp.bfloat16)


def draw_kv_pages(key, part):
    key = jax.random.fold_in(key, 12)
    first = jax.random.fold_in(key, 0)
    base = jax.random.normal(first, (2, PAGES, PAGE, KVH, HD), jnp.float32)
    return jnp.clip(base, -6.0, 6.0).reshape(2, PAGES, PAGE, KVH * HD).astype(jnp.bfloat16)


def draw_context_len(key, part):
    key = jax.random.fold_in(key, 13)
    first, second, third = jax.random.split(key, 3)
    factor = jax.random.randint(first, (N_REQ, 1), 1, 5)
    raw = jax.random.randint(second, (N_REQ, REQ_DEV), 0, MAXLEN)
    lens = (1 + raw % (factor * (MAXLEN // 4))).reshape(R)
    chosen = jax.random.randint(third, (), 0, R)
    lens = jnp.where(jnp.arange(R) == chosen, MAXLEN, lens)
    return lens.astype(jnp.int32)


def steps_of(stream_key, shape, cuts, low, top_value):
    gain, own = 1.0, jax.random.fold_in(stream_key, 6)
    for axis_at, parts in cuts:
        heights = jnp.exp(jax.random.uniform(jax.random.fold_in(own, axis_at), (parts,), jnp.float32, low / len(cuts), top_value / len(cuts)))
        gain = gain * jnp.repeat(heights, shape[axis_at] // parts).reshape([-1 if axis == axis_at else 1 for axis in range(len(shape))])
    return gain


def gaussian(key, shape, deviation, bound, cuts=(), kind=jnp.bfloat16):
    drawn = deviation * jax.random.normal(key, shape, jnp.float32)
    if cuts:
        drawn = drawn * steps_of(key, shape, cuts, -0.22, 0.18)
    return jnp.clip(drawn, -bound, bound).astype(kind)


def setup_inputs(seed: int = 0, part: int = 0) -> dict:
    key_of = jax.random.split(jax.random.key(seed), 18)
    part_keys = jax.random.split(jax.random.fold_in(key_of[17], part), 18)
    ssm_state = gaussian(part_keys[0], (R, STATE, DI), 1.0, 6.0, ((0, 8), (2, 2)), jnp.float32)
    conv_state = gaussian(part_keys[1], (R, CONV - 1, DI), 1.0, 6.0, ((0, 8), (2, 2)), jnp.float32)
    token_input = gaussian(part_keys[2], (R, STEPS, DI), 1.0, 6.0, ((2, 16),))
    gate_input = gaussian(part_keys[3], (R, STEPS, DI), 1.0, 6.0, ((2, 16),))
    conv_weight = gaussian(key_of[4], (CONV, DI), CONV ** -0.5, 3.0, ((1, 2),), jnp.float32)
    conv_bias = gaussian(key_of[5], (DI,), 0.5, 3.0, ((0, 2),), jnp.float32)
    proj_weight = gaussian(key_of[6], (DI, XW), DI ** -0.5, 0.046875, ((0, 16),))
    dt_weight = gaussian(key_of[7], (DT_RANK, DI), DT_RANK ** -0.5, 0.25, ((1, 16),))
    dt_bias = jnp.clip(-3.0 + 3.5 * jax.random.uniform(key_of[8], (DI,), jnp.float32) ** steps_of(key_of[8], (DI,), ((0, 2),), -0.2, 0.2), -3.0, 0.5)
    decay_log = jnp.clip(2.7 * jax.random.uniform(key_of[9], (STATE, DI), jnp.float32) ** steps_of(key_of[9], (STATE, DI), ((1, 2),), -0.2, 0.2), 0.0, 2.7)
    skip_gain = jnp.clip(0.5 + 1.0 * jax.random.uniform(key_of[10], (DI,), jnp.float32) ** steps_of(key_of[10], (DI,), ((0, 2),), -0.2, 0.2), 0.5, 1.5)
    queries = draw_queries(jax.random.fold_in(jax.random.fold_in(key_of[17], part), 71), part)
    kv_pages = draw_kv_pages(jax.random.fold_in(jax.random.fold_in(key_of[17], part), 71), part)
    new_kv = gaussian(part_keys[13], (R, STEPS, 2, KVH * HD), 1.0, 6.0, ((0, 8), (3, 2)))
    page_table = jax.vmap(lambda own: jax.random.permutation(own, PAGES_DEV))(jax.random.split(part_keys[14], N_REQ)).reshape((N_REQ, PAGES_DEV)).astype(jnp.int32)
    context_len = draw_context_len(jax.random.fold_in(jax.random.fold_in(key_of[17], part), 71), part)
    decode_row = jax.random.permutation(part_keys[16], R).astype(jnp.int32)
    return dict(ssm_state=ssm_state, conv_state=conv_state, token_input=token_input, gate_input=gate_input, conv_weight=conv_weight, conv_bias=conv_bias, proj_weight=proj_weight, dt_weight=dt_weight, dt_bias=dt_bias, decay_log=decay_log, skip_gain=skip_gain, queries=queries, kv_pages=kv_pages, new_kv=new_kv, page_table=page_table, context_len=context_len, decode_row=decode_row)


def mamba_rows(states, convs, tokens, gates, conv_weight, conv_bias, proj_weight, dt_weight, dt_bias, decay_log, skip_gain):
    rate = -jnp.exp(decay_log)
    window = jnp.concatenate([convs, tokens.astype(jnp.float32)], axis=1)
    hidden = states
    results = []
    for step in range(STEPS):
        pre = conv_bias + window[:, step] * conv_weight[0]
        for tap in range(1, CONV):
            pre = pre + window[:, step + tap] * conv_weight[tap]
        mixed = jax.nn.silu(pre).astype(jnp.bfloat16)
        proj = jnp.dot(mixed, proj_weight, preferred_element_type=jnp.float32)
        low = proj[:, :DT_RANK].astype(jnp.bfloat16)
        in_map = proj[:, DT_RANK:DT_RANK + STATE]
        out_map = proj[:, DT_RANK + STATE:]
        delta = jax.nn.softplus(jnp.dot(low, dt_weight, preferred_element_type=jnp.float32) + dt_bias)
        inputf = lax.optimization_barrier(mixed).astype(jnp.float32)
        hidden = jnp.exp(delta[:, None, :] * rate[None]) * hidden + delta[:, None, :] * in_map[:, :, None] * inputf[:, None, :]
        value = lax.optimization_barrier(jnp.sum(out_map[:, :, None] * hidden, axis=1)) + skip_gain * inputf
        results.append((value * jax.nn.silu(gates[:, step].astype(jnp.float32))).astype(jnp.bfloat16))
    return jnp.stack(results, axis=1)

def attend(query, key_cache, value_cache, fresh, lens):
    rows = query.shape[0]
    group = HQ // KVH
    scale = 1.0 / math.sqrt(HD)
    qf = query.reshape(rows, STEPS, KVH, group, HD).astype(jnp.float32)
    keys = key_cache.reshape(rows, -1, KVH, HD).astype(jnp.float32)
    values = value_cache.reshape(rows, -1, KVH, HD).astype(jnp.float32)
    new_keys = fresh[:, :, 0].reshape(rows, STEPS, KVH, HD).astype(jnp.float32)
    new_values = fresh[:, :, 1].reshape(rows, STEPS, KVH, HD).astype(jnp.float32)
    old = jnp.einsum('btkgd,bnkd->btkgn', qf, keys) * scale
    new = jnp.einsum('btkgd,bskd->btkgs', qf, new_keys) * scale
    live = jnp.arange(keys.shape[1])[None, :] < lens[:, None]
    causal = jnp.arange(STEPS)[None, :] <= jnp.arange(STEPS)[:, None]
    old = jnp.where(live[:, None, None, None, :], old, -1e+30)
    new = jnp.where(causal[None, :, None, None, :], new, -1e+30)
    top = jnp.maximum(lax.optimization_barrier(jnp.max(old, axis=-1, keepdims=True)), lax.optimization_barrier(jnp.max(new, axis=-1, keepdims=True)))
    exp_old = jnp.exp(old - top)
    exp_new = jnp.exp(new - top)
    total = lax.optimization_barrier(jnp.sum(exp_old, axis=-1, keepdims=True)) + lax.optimization_barrier(jnp.sum(exp_new, axis=-1, keepdims=True))
    w_old = (exp_old / total).astype(jnp.bfloat16).astype(jnp.float32)
    w_new = (exp_new / total).astype(jnp.bfloat16).astype(jnp.float32)
    out = jnp.einsum('btkgn,bnkd->btkgd', w_old, values) + jnp.einsum('btkgs,bskd->btkgd', w_new, new_values)
    return out.reshape(rows, STEPS, HQ * HD).astype(jnp.bfloat16)

def reference(ssm_state, conv_state, token_input, gate_input, conv_weight, conv_bias, proj_weight, dt_weight, dt_bias, decay_log, skip_gain, queries, kv_pages, new_kv, page_table, context_len, decode_row):
    block = math.gcd(R, 64)
    count = R // block
    source = jnp.zeros((R,), jnp.int32).at[decode_row].set(jnp.arange(R, dtype=jnp.int32))
    states = ssm_state[source].reshape(count, block, STATE, DI)
    convs = conv_state[source].reshape(count, block, CONV - 1, DI)
    tokens = token_input.reshape(count, block, STEPS, DI)
    gates = gate_input.reshape(count, block, STEPS, DI)

    def mamba_block(items):
        return mamba_rows(items[0], items[1], items[2], items[3], conv_weight, conv_bias, proj_weight, dt_weight, dt_bias, decay_log, skip_gain)
    mamba_out = lax.map(mamba_block, (states, convs, tokens, gates)).reshape(R, STEPS, DI)
    owner = jnp.arange(R, dtype=jnp.int32) // REQ_DEV
    global_pages = owner[:, None] * PAGES_DEV + page_table.reshape(R, MAXP)

    def attention_block(items):
        query, pages, fresh, lens = items
        rows = query.shape[0]
        key_cache = kv_pages[0][pages].reshape(rows, MAXP * PAGE, KVH * HD)
        value_cache = kv_pages[1][pages].reshape(rows, MAXP * PAGE, KVH * HD)
        return attend(query, key_cache, value_cache, fresh, lens)
    attended = lax.map(attention_block, (queries.reshape(count, block, STEPS, HQ * HD), global_pages.reshape(count, block, MAXP), new_kv.reshape(count, block, STEPS, 2, KVH * HD), context_len.reshape(count, block)))
    attended = attended.reshape(R, STEPS, HQ * HD)
    attention_out = attended[source]
    return (mamba_out, attention_out)
```

```python
import functools
import math

import jax
import jax.numpy as jnp
from jax import lax
from jax.experimental import pallas as pl
from jax.experimental.pallas import tpu as pltpu
from jax.sharding import PartitionSpec as P

STATE = 16
CONV = 4
DT_RANK = 512
HQ = 64
KVH = 8
HD = 128
STEPS = 2


def convolve(convs, tokens, conv_weight, conv_bias):
    window = jnp.concatenate([convs, tokens.astype(jnp.float32)], axis=1)
    results = []
    for step in range(STEPS):
        pre = conv_bias + window[:, step] * conv_weight[0]
        for tap in range(1, CONV):
            pre = pre + window[:, step + tap] * conv_weight[tap]
        results.append(jax.nn.silu(pre).astype(jnp.bfloat16))
    return jnp.stack(results, axis=1)


def project(mixed, proj_weight):
    partial_sum = jnp.einsum("rtc,cx->rtx", mixed, proj_weight, preferred_element_type=jnp.float32)
    return lax.psum(partial_sum, ("req", "tp"))


def step_sizes(proj, dt_weight, bias_cols):
    low = proj[:, :, :DT_RANK].astype(jnp.bfloat16)
    return jax.nn.softplus(
        jnp.einsum("rtk,kc->rtc", low, dt_weight, preferred_element_type=jnp.float32) + bias_cols
    )


def advance(hidden, mixed, delta, proj, gates, decay_log, skip_gain):
    rate = -jnp.exp(decay_log)
    results = []
    for step in range(STEPS):
        in_map = proj[:, step, DT_RANK : DT_RANK + STATE]
        out_map = proj[:, step, DT_RANK + STATE :]
        inputf = lax.optimization_barrier(mixed[:, step]).astype(jnp.float32)
        rates_now = delta[:, step]
        hidden = (
            jnp.exp(rates_now[:, None, :] * rate[None]) * hidden
            + rates_now[:, None, :] * in_map[:, :, None] * inputf[:, None, :]
        )
        value = jnp.sum(out_map[:, :, None] * hidden, axis=1) + skip_gain * inputf
        results.append(
            (value * jax.nn.silu(gates[:, step].astype(jnp.float32))).astype(jnp.bfloat16)
        )
    return jnp.stack(results, axis=1)


def attend(query, key_cache, value_cache, fresh, lens, heads, kv_heads):
    rows = query.shape[0]
    group = heads // kv_heads
    scale = 1.0 / math.sqrt(HD)
    queryq = query.reshape(rows, STEPS, kv_heads, group, HD)
    keys = key_cache.reshape(rows, -1, kv_heads, HD)
    values = value_cache.reshape(rows, -1, kv_heads, HD)
    new_keys = fresh[:, :, 0].reshape(rows, STEPS, kv_heads, HD)
    new_values = fresh[:, :, 1].reshape(rows, STEPS, kv_heads, HD)
    old = jnp.einsum("btkgd,bnkd->btkgn", queryq, keys, preferred_element_type=jnp.float32) * scale
    new = (
        jnp.einsum("btkgd,bskd->btkgs", queryq, new_keys, preferred_element_type=jnp.float32)
        * scale
    )
    live = jnp.arange(keys.shape[1])[None, :] < lens[:, None]
    causal = jnp.arange(STEPS)[None, :] <= jnp.arange(STEPS)[:, None]
    old = jnp.where(live[:, None, None, None, :], old, -1e30)
    new = jnp.where(causal[None, :, None, None, :], new, -1e30)
    top = jnp.maximum(jnp.max(old, axis=-1, keepdims=True), jnp.max(new, axis=-1, keepdims=True))
    exp_old = jnp.exp(old - top)
    exp_new = jnp.exp(new - top)
    total = jnp.sum(exp_old, axis=-1, keepdims=True) + jnp.sum(exp_new, axis=-1, keepdims=True)
    w_old = (exp_old / total).astype(jnp.bfloat16)
    w_new = (exp_new / total).astype(jnp.bfloat16)
    out = jnp.einsum("btkgn,bnkd->btkgd", w_old, values, preferred_element_type=jnp.float32)
    out = out + jnp.einsum(
        "btkgs,bskd->btkgd", w_new, new_values, preferred_element_type=jnp.float32
    )
    return out.reshape(rows, STEPS, heads * HD).astype(jnp.bfloat16)


def local(
    ssm_state,
    conv_state,
    token_input,
    gate_input,
    conv_weight,
    conv_bias,
    proj_weight,
    dt_weight,
    dt_bias,
    decay_log,
    skip_gain,
    queries,
    kv_pages,
    new_kv,
    page_table,
    context_len,
    decode_row,
):
    slots = ssm_state.shape[0]
    total = decode_row.shape[0]
    cols = token_input.shape[2]
    source = jnp.zeros((total,), jnp.int32).at[decode_row].set(jnp.arange(total, dtype=jnp.int32))
    offset = lax.axis_index("req") * cols
    heads = HQ // lax.axis_size("tp")
    kv_heads = KVH // lax.axis_size("tp")
    flat_pages = page_table.reshape(-1)
    key_cache = kv_pages[0][flat_pages].reshape(slots, -1, kv_heads * HD)
    value_cache = kv_pages[1][flat_pages].reshape(slots, -1, kv_heads * HD)
    attended = attend(queries, key_cache, value_cache, new_kv, context_len, heads, kv_heads)
    spread = lax.all_to_all(attended, "req", split_axis=2, concat_axis=0, tiled=True)
    attention_out = spread[source]
    bias_cols = lax.dynamic_slice_in_dim(dt_bias, offset, cols, 0)
    tok_slot, gate_slot = (
        lax.all_to_all(token_input[decode_row], "req", split_axis=0, concat_axis=2, tiled=True),
        lax.all_to_all(gate_input[decode_row], "req", split_axis=0, concat_axis=2, tiled=True),
    )
    mixed_slot = convolve(conv_state, tok_slot, conv_weight, conv_bias)
    mixed_cols = lax.all_to_all(mixed_slot, "req", split_axis=2, concat_axis=0, tiled=True)
    proj = project(mixed_cols, proj_weight)
    delta_cols = step_sizes(proj, dt_weight, bias_cols)
    delta = lax.all_to_all(delta_cols, "req", split_axis=0, concat_axis=2, tiled=True)
    mine = lax.dynamic_slice_in_dim(proj, lax.axis_index("req") * slots, slots, 0)
    result = advance(ssm_state, mixed_slot, delta, mine, gate_slot, decay_log, skip_gain)
    back = lax.all_to_all(result, "req", split_axis=2, concat_axis=0, tiled=True)
    mamba_out = back[source]
    return (mamba_out, attention_out)


ROWS = 16


def block_kernel(
    n,
    slots,
    cols,
    acols,
    kv_heads,
    pre_ref,
    tok_ref,
    gate_ref,
    vec_ref,
    perm_col_ref,
    perm_row_ref,
    query_ref,
    fresh_ref,
    bias_ref,
    fresh_bias_ref,
    state_hbm,
    kv_hbm,
    pw_hbm,
    dtw_hbm,
    decay_hbm,
    mamba_ref,
    att_ref,
    state,
    kv,
    pw,
    dtw,
    decay,
    pre_send,
    pre_recv,
    tok_send,
    tok_recv,
    part_send,
    part_recv,
    low_send,
    low_recv,
    del_send,
    del_recv,
    val_send,
    val_recv,
    att_send,
    att_recv,
    zbuf,
    vbuf,
    maps_t,
    load_sem,
    pre_ss,
    pre_rs,
    tok_ss,
    tok_rs,
    part_ss,
    part_rs,
    low_ss,
    low_rs,
    del_ss,
    del_rs,
    val_ss,
    val_rs,
    att_ss,
    att_rs,
):
    me = lax.axis_index("req")
    core = lax.axis_index("tp")
    total = 2 * n
    flat = core * n + me
    rows = n * ROWS
    f32, bf16 = jnp.float32, jnp.bfloat16

    loads = [
        pltpu.make_async_copy(src, dst, load_sem.at[i])
        for i, (src, dst) in enumerate(
            ((kv_hbm, kv), (pw_hbm, pw), (dtw_hbm, dtw), (state_hbm, state), (decay_hbm, decay))
        )
    ]
    for load in loads:
        load.start()

    barrier = pltpu.get_barrier_semaphore()

    @pl.loop(1, total)
    def _(k):
        other = lax.rem(flat + k, total)
        pl.semaphore_signal(
            barrier,
            inc=1,
            device_id={"req": lax.rem(other, n), "tp": other // n},
            device_id_type=pl.DeviceIdType.MESH,
        )

    def req_copy(src, dst, ss, rs, peer, slot):
        return pltpu.make_async_remote_copy(
            src_ref=src.at[peer],
            dst_ref=dst.at[slot],
            send_sem=ss.at[peer],
            recv_sem=rs.at[slot],
            device_id={"req": peer, "tp": core},
            device_id_type=pl.DeviceIdType.MESH,
        )

    def req_start(src, dst, ss, rs):
        @pl.loop(1, n)
        def _(k):
            peer = lax.rem(me + k, n)
            req_copy(src, dst, ss, rs, peer, me).start()

    def req_wait(src, dst, ss, rs):
        @pl.loop(1, n)
        def _(k):
            peer = lax.rem(me + k, n)
            req_copy(src, dst, ss, rs, peer, peer).wait_recv()

    def req_drain(src, dst, ss, rs):
        @pl.loop(1, n)
        def _(k):
            peer = lax.rem(me + k, n)
            req_copy(src, dst, ss, rs, peer, me).wait_send()

    def all_copy(src, dst, ss, rs, peer, slot):
        return pltpu.make_async_remote_copy(
            src_ref=src,
            dst_ref=dst.at[slot],
            send_sem=ss.at[peer],
            recv_sem=rs.at[slot],
            device_id={"req": lax.rem(peer, n), "tp": peer // n},
            device_id_type=pl.DeviceIdType.MESH,
        )

    for j in range(n):
        pre_send[j] = pre_ref[:, j * cols : (j + 1) * cols].astype(bf16)
    lane = lax.broadcasted_iota(jnp.int32, (rows, rows), 1)
    perm = jnp.where(perm_col_ref[...] == lane, 1.0, 0.0).astype(bf16)
    tok = jnp.dot(perm, tok_ref[...], preferred_element_type=f32)
    tok_send[...] = tok.astype(bf16).reshape(n, ROWS, cols)

    pl.semaphore_wait(barrier, total - 1)
    req_start(pre_send, pre_recv, pre_ss, pre_rs)
    req_start(tok_send, tok_recv, tok_ss, tok_rs)
    pre_recv[pl.ds(me, 1)] = pre_send[pl.ds(me, 1)]
    tok_recv[pl.ds(me, 1)] = tok_send[pl.ds(me, 1)]

    loads[0].wait()
    group = (acols * n) // (kv_heads * HD)
    per_block = acols // HD
    scale = 1.0 / math.sqrt(HD)
    contract = (((1,), (1,)), ((), ()))

    @pl.loop(0, kv_heads)
    def _(h):
        lanes = pl.ds(pl.multiple_of(h * HD, HD), HD)
        q = jnp.concatenate(
            [
                query_ref[:, pl.ds(pl.multiple_of((h * group + g) * HD, HD), HD)]
                for g in range(group)
            ],
            axis=0,
        )
        old = lax.dot_general(q, kv[0, :, lanes], contract, preferred_element_type=f32)
        new = lax.dot_general(
            q, fresh_ref[0, :, lanes], contract, preferred_element_type=f32
        )
        old = old.reshape(group, ROWS, -1) * scale + bias_ref[...][None]
        new = new.reshape(group, ROWS, -1) * scale + fresh_bias_ref[...][None]
        top = jnp.maximum(
            jnp.max(old, axis=-1, keepdims=True), jnp.max(new, axis=-1, keepdims=True)
        )
        old = jnp.exp(old - top)
        new = jnp.exp(new - top)
        norm = jnp.sum(old, axis=-1, keepdims=True) + jnp.sum(new, axis=-1, keepdims=True)
        old = old.astype(bf16).reshape(group * ROWS, -1)
        new = new.astype(bf16).reshape(group * ROWS, -1)
        out = jnp.dot(old, kv[1, :, lanes], preferred_element_type=f32)
        out = out + jnp.dot(new, fresh_ref[1, :, lanes], preferred_element_type=f32)
        out = (out.reshape(group, ROWS, HD) / norm).astype(bf16)
        for g in range(group):
            place = g % per_block
            att_send[h * (group // per_block) + g // per_block, :, place * HD : (place + 1) * HD] = out[g]

    here = pl.ds(pl.multiple_of(me * cols, cols), cols)
    taps = vec_ref[0:2, here]
    bias_cols = vec_ref[2:3, here]
    tok4 = tok.reshape(n, 2, 8, cols)
    req_wait(pre_send, pre_recv, pre_ss, pre_rs)
    pre4 = pre_recv[...].astype(f32).reshape(n, 2, 8, cols)
    first = pre4[:, 0] + tok4[:, 0] * taps[1:2][None]
    second = pre4[:, 1] + tok4[:, 0] * taps[0:1][None] + tok4[:, 1] * taps[1:2][None]
    mixed = jnp.stack([jax.nn.silu(first), jax.nn.silu(second)], axis=1)
    mixed = mixed.reshape(rows, cols).astype(bf16)
    loads[1].wait()
    part = jnp.dot(mixed, pw[...], preferred_element_type=f32)
    half = DT_RANK // 2
    maps = jnp.concatenate(
        [part[:, DT_RANK:], jnp.zeros((rows, 128 - 2 * STATE), f32)], axis=1
    )
    for c in range(2):
        part_send[c * n : (c + 1) * n, :, :half] = (
            part[:, c * half : (c + 1) * half].astype(bf16).reshape(n, ROWS, half)
        )
        part_send[c * n : (c + 1) * n, :, half:] = maps.astype(bf16).reshape(n, ROWS, 128)

    @pl.loop(1, total)
    def _(k):
        peer = lax.rem(flat + k, total)
        all_copy(part_send.at[peer], part_recv, part_ss, part_rs, peer, flat).start()

    part_recv[pl.ds(flat, 1)] = part_send[pl.ds(flat, 1)]

    @pl.loop(1, total)
    def _(k):
        peer = lax.rem(flat + k, total)
        all_copy(part_send.at[peer], part_recv, part_ss, part_rs, peer, peer).wait_recv()

    summed = jnp.sum(part_recv[...].astype(f32), axis=0)
    low_send[...] = summed[:, :half].astype(bf16)

    @pl.loop(1, total)
    def _(k):
        peer = lax.rem(flat + k, total)
        all_copy(low_send, low_recv, low_ss, low_rs, peer, flat).start()

    low_recv[pl.ds(flat, 1)] = low_send[...][None]
    req_start(att_send, att_recv, att_ss, att_rs)
    att_recv[pl.ds(me, 1)] = att_send[pl.ds(me, 1)]
    square = jnp.concatenate(
        [summed[:, half:], jnp.zeros((128 - ROWS, 128), f32)], axis=0
    )
    maps_t[...] = jnp.transpose(square)[: 2 * STATE]
    loads[2].wait()

    @pl.loop(1, total)
    def _(k):
        peer = lax.rem(flat + k, total)
        all_copy(low_send, low_recv, low_ss, low_rs, peer, peer).wait_recv()

    z = jnp.dot(low_recv[:n].reshape(rows, half), dtw[:half], preferred_element_type=f32)
    z = z + jnp.dot(low_recv[n:].reshape(rows, half), dtw[half:], preferred_element_type=f32)
    zbuf[...] = (z + bias_cols).reshape(n, ROWS, cols)

    @pl.loop(0, n)
    def _(k):
        peer = lax.rem(me + 1 + k, n)
        block = zbuf[pl.ds(peer, 1)]
        delta = jnp.maximum(block, 0.0) + jnp.log1p(jnp.exp(-jnp.abs(block)))
        del_send[pl.ds(peer, 1)] = delta.astype(bf16)

        @pl.when(k < n - 1)
        def _():
            req_copy(del_send, del_recv, del_ss, del_rs, peer, me).start()

    del_recv[pl.ds(me, 1)] = del_send[pl.ds(me, 1)]
    loads[3].wait()
    loads[4].wait()
    req_wait(tok_send, tok_recv, tok_ss, tok_rs)

    @pl.loop(0, n)
    def _(k):
        peer = lax.rem(me - k + n, n)

        @pl.when(k > 0)
        def _():
            req_copy(del_send, del_recv, del_ss, del_rs, peer, peer).wait_recv()

        block = pl.ds(pl.multiple_of(peer * cols, cols), cols)
        delta = del_recv[peer].astype(f32)
        toks = tok_recv[peer].astype(f32)
        w2 = vec_ref[0:1, block]
        w3 = vec_ref[1:2, block]
        skip = vec_ref[3:4, block]
        x0 = pre_ref[0:8, block] + toks[0:8] * w3
        x1 = pre_ref[8:16, block] + toks[0:8] * w2 + toks[8:16] * w3
        x = jnp.concatenate([jax.nn.silu(x0), jax.nn.silu(x1)], axis=0)
        x = x.astype(bf16).astype(f32)
        dx = delta * x
        rate = -jnp.exp(decay[:, block])
        for s in range(slots):
            h = state[s, :, block]
            for t in range(STEPS):
                i = t * slots + s
                h = jnp.exp(delta[i : i + 1] * rate) * h + dx[i : i + 1] * maps_t[:STATE, i : i + 1]
                vbuf[i : i + 1, :] = jnp.sum(
                    h * maps_t[STATE:, i : i + 1], axis=0, keepdims=True
                )
        val_send[peer] = (vbuf[...] + skip * x).astype(bf16)

        @pl.when(k > 0)
        def _():
            req_copy(val_send, val_recv, val_ss, val_rs, peer, me).start()

    val_recv[pl.ds(me, 1)] = val_send[pl.ds(me, 1)]

    sub = lax.broadcasted_iota(jnp.int32, (rows, rows), 0)
    back = jnp.where(perm_row_ref[...] == sub, 1.0, 0.0).astype(bf16)
    gate = jax.nn.silu(gate_ref[...].astype(f32))
    req_wait(att_send, att_recv, att_ss, att_rs)
    att = jnp.dot(back, att_recv[...].reshape(rows, acols), preferred_element_type=f32)
    att_ref[...] = att.astype(bf16)
    req_wait(val_send, val_recv, val_ss, val_rs)
    val = jnp.dot(back, val_recv[...].reshape(rows, cols), preferred_element_type=f32)
    mamba_ref[...] = (val * gate).astype(bf16)

    req_drain(pre_send, pre_recv, pre_ss, pre_rs)
    req_drain(tok_send, tok_recv, tok_ss, tok_rs)
    req_drain(att_send, att_recv, att_ss, att_rs)
    req_drain(del_send, del_recv, del_ss, del_rs)
    req_drain(val_send, val_recv, val_ss, val_rs)

    @pl.loop(1, total)
    def _(k):
        peer = lax.rem(flat + k, total)
        all_copy(part_send.at[peer], part_recv, part_ss, part_rs, peer, flat).wait_send()
        all_copy(low_send, low_recv, low_ss, low_rs, peer, flat).wait_send()


def local_kernel(
    ssm_state,
    conv_state,
    token_input,
    gate_input,
    conv_weight,
    conv_bias,
    proj_weight,
    dt_weight,
    dt_bias,
    decay_log,
    skip_gain,
    queries,
    kv_pages,
    new_kv,
    page_table,
    context_len,
    decode_row,
):
    n = lax.axis_size("req")
    slots = ssm_state.shape[0]
    width = ssm_state.shape[2]
    total = decode_row.shape[0]
    cols = token_input.shape[2]
    acols = queries.shape[2] // n
    kv_heads = KVH // lax.axis_size("tp")
    pages, page = kv_pages.shape[1:3]
    per_slot = pages // slots
    rows = total * STEPS
    pre0 = (
        conv_bias
        + conv_state[:, 0] * conv_weight[0]
        + conv_state[:, 1] * conv_weight[1]
        + conv_state[:, 2] * conv_weight[2]
    )
    pre1 = conv_bias + conv_state[:, 1] * conv_weight[0] + conv_state[:, 2] * conv_weight[1]
    pre = jnp.concatenate([pre0, pre1], axis=0)
    vecs = jnp.concatenate([conv_weight[2:4], dt_bias[None], skip_gain[None]], axis=0)
    target = (
        decode_row.reshape(n, 1, slots) * STEPS + jnp.arange(STEPS, dtype=jnp.int32)[None, :, None]
    ).reshape(rows)
    entry = jnp.sum(
        jnp.where(
            page_table.reshape(-1, 1) == jnp.arange(pages)[None],
            jnp.arange(pages, dtype=jnp.int32)[:, None],
            0,
        ),
        axis=0,
    )
    place = (entry % per_slot)[:, None] * page + jnp.arange(page)[None]
    limit = jnp.where(
        (entry // per_slot)[None] == jnp.arange(slots)[:, None], context_len[:, None], 0
    )
    live = (place[None] < limit[:, :, None]).reshape(slots, pages * page)
    bias = jnp.where(live, 0.0, -1e30).astype(jnp.float32)
    bias = jnp.concatenate([bias] * STEPS, axis=0)
    index = jnp.arange(STEPS * slots)
    own = (index % slots)[:, None] == (index % slots)[None]
    causal = (index // slots)[None] <= (index // slots)[:, None]
    fresh_bias = jnp.where(own & causal, 0.0, -1e30).astype(jnp.float32)
    query_rows = queries.transpose(1, 0, 2).reshape(STEPS * slots, -1)
    fresh = new_kv.transpose(2, 1, 0, 3).reshape(2, STEPS * slots, -1)
    kv = kv_pages.reshape(2, pages * page, -1)
    half = DT_RANK // 2
    bf16, f32 = jnp.bfloat16, jnp.float32
    vmem = pl.BlockSpec(memory_space=pltpu.VMEM)
    hbm = pl.BlockSpec(memory_space=pl.ANY)
    dma = pltpu.SemaphoreType.DMA
    mamba, attended = pl.pallas_call(
        functools.partial(block_kernel, n, slots, cols, acols, kv_heads),
        out_shape=(
            jax.ShapeDtypeStruct((rows, cols), bf16),
            jax.ShapeDtypeStruct((rows, acols), bf16),
        ),
        in_specs=[vmem] * 10 + [hbm] * 5,
        out_specs=(vmem, vmem),
        scratch_shapes=[
            pltpu.VMEM(ssm_state.shape, f32),
            pltpu.VMEM(kv.shape, bf16),
            pltpu.VMEM(proj_weight.shape, bf16),
            pltpu.VMEM(dt_weight.shape, bf16),
            pltpu.VMEM(decay_log.shape, f32),
            pltpu.VMEM((n, ROWS, cols), bf16),
            pltpu.VMEM((n, ROWS, cols), bf16),
            pltpu.VMEM((n, ROWS, cols), bf16),
            pltpu.VMEM((n, ROWS, cols), bf16),
            pltpu.VMEM((2 * n, ROWS, half + 128), bf16),
            pltpu.VMEM((2 * n, ROWS, half + 128), bf16),
            pltpu.VMEM((ROWS, half), bf16),
            pltpu.VMEM((2 * n, ROWS, half), bf16),
            pltpu.VMEM((n, ROWS, cols), bf16),
            pltpu.VMEM((n, ROWS, cols), bf16),
            pltpu.VMEM((n, ROWS, cols), bf16),
            pltpu.VMEM((n, ROWS, cols), bf16),
            pltpu.VMEM((n, ROWS, acols), bf16),
            pltpu.VMEM((n, ROWS, acols), bf16),
            pltpu.VMEM((n, ROWS, cols), f32),
            pltpu.VMEM((ROWS, cols), f32),
            pltpu.VMEM((2 * STATE, 128), f32),
            dma((5,)),
            dma((n,)),
            dma((n,)),
            dma((n,)),
            dma((n,)),
            dma((2 * n,)),
            dma((2 * n,)),
            dma((2 * n,)),
            dma((2 * n,)),
            dma((n,)),
            dma((n,)),
            dma((n,)),
            dma((n,)),
            dma((n,)),
            dma((n,)),
        ],
        compiler_params=pltpu.CompilerParams(
            collective_id=0, has_side_effects=True, vmem_limit_bytes=44 * 2**20
        ),
    )(
        pre,
        token_input.reshape(rows, cols),
        gate_input.reshape(rows, cols),
        vecs,
        target[:, None],
        target[None],
        query_rows,
        fresh,
        bias,
        fresh_bias,
        ssm_state,
        kv,
        proj_weight,
        dt_weight,
        decay_log,
    )
    return mamba.reshape(total, STEPS, cols), attended.reshape(total, STEPS, acols)


def solution(mesh):
    in_specs = (
        P(("groups", "req"), None, "tp"),
        P(("groups", "req"), None, "tp"),
        P("groups", None, ("tp", "req")),
        P("groups", None, ("tp", "req")),
        P(None, "tp"),
        P("tp"),
        P(("tp", "req"), None),
        P(None, ("tp", "req")),
        P("tp"),
        P(None, "tp"),
        P("tp"),
        P(("groups", "req"), None, "tp"),
        P(None, ("groups", "req"), None, "tp"),
        P(("groups", "req"), None, None, "tp"),
        P(("groups", "req"), None),
        P(("groups", "req")),
        P("groups"),
    )
    out_specs = (P("groups", None, ("tp", "req")), P("groups", None, ("tp", "req")))
    kernel_fits = mesh.shape["req"] <= 8 and mesh.shape["tp"] == 2
    body = local_kernel if kernel_fits else local
    return jax.shard_map(body, mesh=mesh, in_specs=in_specs, out_specs=out_specs, check_vma=False)
```

```python
import functools
import math

import jax
import jax.numpy as jnp
from jax import lax
from jax.experimental import pallas as pl
from jax.experimental.pallas import tpu as pltpu
from jax.sharding import PartitionSpec as P

STATE = 16
CONV = 4
DT_RANK = 512
HQ = 64
KVH = 8
HD = 128
STEPS = 2


def convolve(convs, tokens, conv_weight, conv_bias):
    window = jnp.concatenate([convs, tokens.astype(jnp.float32)], axis=1)
    results = []
    for step in range(STEPS):
        pre = conv_bias + window[:, step] * conv_weight[0]
        for tap in range(1, CONV):
            pre = pre + window[:, step + tap] * conv_weight[tap]
        results.append(jax.nn.silu(pre).astype(jnp.bfloat16))
    return jnp.stack(results, axis=1)


def project(mixed, proj_weight):
    partial_sum = jnp.einsum("rtc,cx->rtx", mixed, proj_weight, preferred_element_type=jnp.float32)
    return lax.psum(partial_sum, ("req", "tp"))


def step_sizes(proj, dt_weight, bias_cols):
    low = proj[:, :, :DT_RANK].astype(jnp.bfloat16)
    return jax.nn.softplus(
        jnp.einsum("rtk,kc->rtc", low, dt_weight, preferred_element_type=jnp.float32) + bias_cols
    )


def advance(hidden, mixed, delta, proj, gates, decay_log, skip_gain):
    rate = -jnp.exp(decay_log)
    results = []
    for step in range(STEPS):
        in_map = proj[:, step, DT_RANK : DT_RANK + STATE]
        out_map = proj[:, step, DT_RANK + STATE :]
        inputf = lax.optimization_barrier(mixed[:, step]).astype(jnp.float32)
        rates_now = delta[:, step]
        hidden = (
            jnp.exp(rates_now[:, None, :] * rate[None]) * hidden
            + rates_now[:, None, :] * in_map[:, :, None] * inputf[:, None, :]
        )
        value = jnp.sum(out_map[:, :, None] * hidden, axis=1) + skip_gain * inputf
        results.append(
            (value * jax.nn.silu(gates[:, step].astype(jnp.float32))).astype(jnp.bfloat16)
        )
    return jnp.stack(results, axis=1)


def attend(query, key_cache, value_cache, fresh, lens, heads, kv_heads):
    rows = query.shape[0]
    group = heads // kv_heads
    scale = 1.0 / math.sqrt(HD)
    queryq = query.reshape(rows, STEPS, kv_heads, group, HD)
    keys = key_cache.reshape(rows, -1, kv_heads, HD)
    values = value_cache.reshape(rows, -1, kv_heads, HD)
    new_keys = fresh[:, :, 0].reshape(rows, STEPS, kv_heads, HD)
    new_values = fresh[:, :, 1].reshape(rows, STEPS, kv_heads, HD)
    old = jnp.einsum("btkgd,bnkd->btkgn", queryq, keys, preferred_element_type=jnp.float32) * scale
    new = (
        jnp.einsum("btkgd,bskd->btkgs", queryq, new_keys, preferred_element_type=jnp.float32)
        * scale
    )
    live = jnp.arange(keys.shape[1])[None, :] < lens[:, None]
    causal = jnp.arange(STEPS)[None, :] <= jnp.arange(STEPS)[:, None]
    old = jnp.where(live[:, None, None, None, :], old, -1e30)
    new = jnp.where(causal[None, :, None, None, :], new, -1e30)
    top = jnp.maximum(jnp.max(old, axis=-1, keepdims=True), jnp.max(new, axis=-1, keepdims=True))
    exp_old = jnp.exp(old - top)
    exp_new = jnp.exp(new - top)
    total = jnp.sum(exp_old, axis=-1, keepdims=True) + jnp.sum(exp_new, axis=-1, keepdims=True)
    w_old = (exp_old / total).astype(jnp.bfloat16)
    w_new = (exp_new / total).astype(jnp.bfloat16)
    out = jnp.einsum("btkgn,bnkd->btkgd", w_old, values, preferred_element_type=jnp.float32)
    out = out + jnp.einsum(
        "btkgs,bskd->btkgd", w_new, new_values, preferred_element_type=jnp.float32
    )
    return out.reshape(rows, STEPS, heads * HD).astype(jnp.bfloat16)


def local(
    ssm_state,
    conv_state,
    token_input,
    gate_input,
    conv_weight,
    conv_bias,
    proj_weight,
    dt_weight,
    dt_bias,
    decay_log,
    skip_gain,
    queries,
    kv_pages,
    new_kv,
    page_table,
    context_len,
    decode_row,
):
    slots = ssm_state.shape[0]
    total = decode_row.shape[0]
    cols = token_input.shape[2]
    source = jnp.zeros((total,), jnp.int32).at[decode_row].set(jnp.arange(total, dtype=jnp.int32))
    offset = lax.axis_index("req") * cols
    heads = HQ // lax.axis_size("tp")
    kv_heads = KVH // lax.axis_size("tp")
    flat_pages = page_table.reshape(-1)
    key_cache = kv_pages[0][flat_pages].reshape(slots, -1, kv_heads * HD)
    value_cache = kv_pages[1][flat_pages].reshape(slots, -1, kv_heads * HD)
    attended = attend(queries, key_cache, value_cache, new_kv, context_len, heads, kv_heads)
    spread = lax.all_to_all(attended, "req", split_axis=2, concat_axis=0, tiled=True)
    attention_out = spread[source]
    bias_cols = lax.dynamic_slice_in_dim(dt_bias, offset, cols, 0)
    tok_slot, gate_slot = (
        lax.all_to_all(token_input[decode_row], "req", split_axis=0, concat_axis=2, tiled=True),
        lax.all_to_all(gate_input[decode_row], "req", split_axis=0, concat_axis=2, tiled=True),
    )
    mixed_slot = convolve(conv_state, tok_slot, conv_weight, conv_bias)
    mixed_cols = lax.all_to_all(mixed_slot, "req", split_axis=2, concat_axis=0, tiled=True)
    proj = project(mixed_cols, proj_weight)
    delta_cols = step_sizes(proj, dt_weight, bias_cols)
    delta = lax.all_to_all(delta_cols, "req", split_axis=0, concat_axis=2, tiled=True)
    mine = lax.dynamic_slice_in_dim(proj, lax.axis_index("req") * slots, slots, 0)
    result = advance(ssm_state, mixed_slot, delta, mine, gate_slot, decay_log, skip_gain)
    back = lax.all_to_all(result, "req", split_axis=2, concat_axis=0, tiled=True)
    mamba_out = back[source]
    return (mamba_out, attention_out)


ROWS = 16


def block_kernel(
    n,
    slots,
    cols,
    acols,
    kv_heads,
    kv_hbm,
    query_hbm,
    fresh_hbm,
    pw_hbm,
    dtw_hbm,
    state_hbm,
    decay_hbm,
    gate_hbm,
    dt_bias_hbm,
    skip_hbm,
    conv_hbm,
    taps_hbm,
    conv_bias_hbm,
    tok_hbm,
    row_ref,
    table_ref,
    len_ref,
    mamba_ref,
    att_ref,
    kv,
    query_in,
    fresh_in,
    pw,
    dtw,
    state,
    decay,
    gate_in,
    dt_bias,
    skip_gain,
    conv,
    taps,
    conv_bias,
    tok_in,
    pre,
    bias,
    query,
    fresh_ref,
    pre_send,
    pre_recv,
    tok_send,
    tok_recv,
    part_send,
    part_recv,
    low_send,
    low_recv,
    del_send,
    del_recv,
    val_send,
    val_recv,
    att_send,
    att_recv,
    zbuf,
    vbuf,
    maps_t,
    load_sem,
    pre_ss,
    pre_rs,
    tok_ss,
    tok_rs,
    part_ss,
    part_rs,
    low_ss,
    low_rs,
    del_ss,
    del_rs,
    val_ss,
    val_rs,
    att_ss,
    att_rs,
):
    me = lax.axis_index("req")
    core = lax.axis_index("tp")
    total = 2 * n
    flat = core * n + me
    rows = n * ROWS
    f32, bf16 = jnp.float32, jnp.bfloat16

    pairs = (
        (conv_hbm, conv),
        (taps_hbm, taps),
        (conv_bias_hbm, conv_bias),
        (tok_hbm, tok_in),
        (query_hbm, query_in),
        (fresh_hbm, fresh_in),
        (kv_hbm, kv),
        (pw_hbm, pw),
        (dt_bias_hbm, dt_bias),
        (dtw_hbm, dtw),
        (state_hbm, state),
        (decay_hbm, decay),
        (skip_hbm, skip_gain),
        (gate_hbm, gate_in),
    )
    loads = [
        pltpu.make_async_copy(src, dst, load_sem.at[i]) for i, (src, dst) in enumerate(pairs)
    ]
    for load in loads:
        load.start()

    barrier = pltpu.get_barrier_semaphore()

    @pl.loop(1, total)
    def _(k):
        other = lax.rem(flat + k, total)
        pl.semaphore_signal(
            barrier,
            inc=1,
            device_id={"req": lax.rem(other, n), "tp": other // n},
            device_id_type=pl.DeviceIdType.MESH,
        )

    def req_copy(src, dst, ss, rs, peer, slot):
        return pltpu.make_async_remote_copy(
            src_ref=src.at[peer],
            dst_ref=dst.at[slot],
            send_sem=ss.at[peer],
            recv_sem=rs.at[slot],
            device_id={"req": peer, "tp": core},
            device_id_type=pl.DeviceIdType.MESH,
        )

    def req_start(src, dst, ss, rs):
        @pl.loop(1, n)
        def _(k):
            peer = lax.rem(me + k, n)
            req_copy(src, dst, ss, rs, peer, me).start()

    def req_wait(src, dst, ss, rs):
        @pl.loop(1, n)
        def _(k):
            peer = lax.rem(me + k, n)
            req_copy(src, dst, ss, rs, peer, peer).wait_recv()

    def req_drain(src, dst, ss, rs):
        @pl.loop(1, n)
        def _(k):
            peer = lax.rem(me + k, n)
            req_copy(src, dst, ss, rs, peer, me).wait_send()

    def all_copy(src, dst, ss, rs, peer, slot):
        return pltpu.make_async_remote_copy(
            src_ref=src,
            dst_ref=dst.at[slot],
            send_sem=ss.at[peer],
            recv_sem=rs.at[slot],
            device_id={"req": lax.rem(peer, n), "tp": peer // n},
            device_id_type=pl.DeviceIdType.MESH,
        )

    for load in loads[:3]:
        load.wait()

    @pl.loop(0, n)
    def _(j):
        block = pl.ds(pl.multiple_of(j * cols, cols), cols)
        w = [taps[i : i + 1, block] for i in range(CONV)]
        oldest, older, last = conv[0, :, block], conv[1, :, block], conv[2, :, block]
        base = conv_bias[:, block]
        first = base + oldest * w[0] + older * w[1] + last * w[2]
        second = base + older * w[0] + last * w[1]
        both = jnp.concatenate([first, second], axis=0)
        pre[:, block] = both
        pre_send[pl.ds(j, 1)] = both.astype(bf16)[None]

    def iota(shape, axis):
        return lax.broadcasted_iota(jnp.int32, shape, axis)

    def hot(condition):
        return jnp.where(condition, 1.0, 0.0).astype(bf16)

    requests = n * slots
    where_row = hot(row_ref[...] == iota((rows, requests), 0) // STEPS)
    column = iota((requests, rows), 1)
    slot_of = column // ROWS * slots + column % slots
    spread = hot(slot_of == iota((requests, rows), 0))
    same_step = iota((rows, rows), 1) % ROWS // slots == iota((rows, rows), 0) % STEPS
    back = jnp.dot(where_row, spread, preferred_element_type=f32)
    back = jnp.where(same_step, back, 0.0).astype(bf16)
    loads[3].wait()
    tok = lax.dot_general(
        back,
        tok_in[...].reshape(rows, cols),
        (((0,), (0,)), ((), ())),
        preferred_element_type=f32,
    )
    tok_send[...] = tok.astype(bf16).reshape(n, ROWS, cols)

    pl.semaphore_wait(barrier, total - 1)
    req_start(pre_send, pre_recv, pre_ss, pre_rs)
    req_start(tok_send, tok_recv, tok_ss, tok_rs)
    pre_recv[pl.ds(me, 1)] = pre_send[pl.ds(me, 1)]
    tok_recv[pl.ds(me, 1)] = tok_send[pl.ds(me, 1)]

    pages = table_ref.shape[1]
    page = kv.shape[1] // pages
    per_slot = pages // slots
    lens = jnp.sum(
        jnp.where(
            iota((slots, slots), 0) == iota((slots, slots), 1), len_ref[...].astype(f32), 0.0
        ),
        axis=1,
        keepdims=True,
    )
    entry = iota((slots, pages), 1)
    counts = lens - (entry % per_slot * page).astype(f32)
    counts = jnp.where(
        entry // per_slot == iota((slots, pages), 0), jnp.clip(counts, 0.0, float(page)), 0.0
    )
    held = hot(table_ref[...] == iota((pages, pages), 0))
    counts = lax.dot_general(
        counts.astype(bf16), held, (((1,), (1,)), ((), ())), preferred_element_type=f32
    )
    widen = hot(iota((pages, pages * page), 1) // page == iota((pages, pages * page), 0))
    counts = jnp.dot(counts.astype(bf16), widen, preferred_element_type=f32)
    token = (iota((slots, pages * page), 1) % page).astype(f32)
    live = jnp.where(token < counts, 0.0, -1e30)
    bias[...] = jnp.concatenate([live] * STEPS, axis=0)
    turned = (iota((ROWS, ROWS), 0) % slots) * STEPS + iota((ROWS, ROWS), 0) // slots
    turn = hot(turned == iota((ROWS, ROWS), 1))
    for load in loads[4:7]:
        load.wait()
    query[...] = jnp.dot(
        turn, query_in[...].reshape(ROWS, -1), preferred_element_type=f32
    ).astype(bf16)
    row32, col32 = iota((2 * ROWS, 2 * ROWS), 0), iota((2 * ROWS, 2 * ROWS), 1)
    pick = (row32 % slots) * 2 * STEPS + (row32 % ROWS) // slots * 2 + row32 // ROWS
    fresh = jnp.dot(
        hot(pick == col32),
        fresh_in[...].reshape(2 * ROWS, -1),
        preferred_element_type=f32,
    ).astype(bf16)
    row16, col16 = iota((ROWS, ROWS), 0), iota((ROWS, ROWS), 1)
    allowed = (row16 % slots == col16 % slots) & (col16 // slots <= row16 // slots)
    fresh_bias = jnp.where(allowed, 0.0, -1e30)
    fresh_ref[...] = fresh.reshape(2, ROWS, -1)
    group = (acols * n) // (kv_heads * HD)
    per_block = acols // HD
    scale = 1.0 / math.sqrt(HD)
    contract = (((1,), (1,)), ((), ()))

    @pl.loop(0, kv_heads)
    def _(h):
        lanes = pl.ds(pl.multiple_of(h * HD, HD), HD)
        q = jnp.concatenate(
            [
                query[:, pl.ds(pl.multiple_of((h * group + g) * HD, HD), HD)]
                for g in range(group)
            ],
            axis=0,
        )
        old = lax.dot_general(q, kv[0, :, lanes], contract, preferred_element_type=f32)
        new = lax.dot_general(
            q, fresh_ref[0, :, lanes], contract, preferred_element_type=f32
        )
        old = old.reshape(group, ROWS, -1) * scale + bias[...][None]
        new = new.reshape(group, ROWS, -1) * scale + fresh_bias[None]
        top = jnp.maximum(
            jnp.max(old, axis=-1, keepdims=True), jnp.max(new, axis=-1, keepdims=True)
        )
        old = jnp.exp(old - top)
        new = jnp.exp(new - top)
        norm = jnp.sum(old, axis=-1, keepdims=True) + jnp.sum(new, axis=-1, keepdims=True)
        old = old.astype(bf16).reshape(group * ROWS, -1)
        new = new.astype(bf16).reshape(group * ROWS, -1)
        out = jnp.dot(old, kv[1, :, lanes], preferred_element_type=f32)
        out = out + jnp.dot(new, fresh_ref[1, :, lanes], preferred_element_type=f32)
        out = (out.reshape(group, ROWS, HD) / norm).astype(bf16)
        for g in range(group):
            place = g % per_block
            att_send[h * (group // per_block) + g // per_block, :, place * HD : (place + 1) * HD] = out[g]

    here = pl.ds(pl.multiple_of(me * cols, cols), cols)
    w2, w3 = taps[2:3, here], taps[3:4, here]
    tok4 = tok.reshape(n, 2, 8, cols)
    req_wait(pre_send, pre_recv, pre_ss, pre_rs)
    pre4 = pre_recv[...].astype(f32).reshape(n, 2, 8, cols)
    first = pre4[:, 0] + tok4[:, 0] * w3[None]
    second = pre4[:, 1] + tok4[:, 0] * w2[None] + tok4[:, 1] * w3[None]
    mixed = jnp.stack([jax.nn.silu(first), jax.nn.silu(second)], axis=1)
    mixed = mixed.reshape(rows, cols).astype(bf16)
    loads[7].wait()
    part = lax.dot_general(mixed, pw[...], contract, preferred_element_type=f32)
    half = DT_RANK // 2
    maps = part[:, DT_RANK:]
    upper = maps.astype(bf16).astype(f32)
    maps = jnp.concatenate(
        [upper, maps - upper, jnp.zeros((rows, 128 - 4 * STATE), f32)], axis=1
    )
    for c in range(2):
        part_send[c * n : (c + 1) * n, :, :half] = (
            part[:, c * half : (c + 1) * half].astype(bf16).reshape(n, ROWS, half)
        )
        part_send[c * n : (c + 1) * n, :, half:] = maps.astype(bf16).reshape(n, ROWS, 128)

    @pl.loop(1, total)
    def _(k):
        peer = lax.rem(flat + k, total)
        all_copy(part_send.at[peer], part_recv, part_ss, part_rs, peer, flat).start()

    part_recv[pl.ds(flat, 1)] = part_send[pl.ds(flat, 1)]

    @pl.loop(1, total)
    def _(k):
        peer = lax.rem(flat + k, total)
        all_copy(part_send.at[peer], part_recv, part_ss, part_rs, peer, peer).wait_recv()

    summed = jnp.sum(part_recv[...].astype(f32), axis=0)
    low_send[...] = summed[:, :half].astype(bf16)

    @pl.loop(1, total)
    def _(k):
        peer = lax.rem(flat + k, total)
        all_copy(low_send, low_recv, low_ss, low_rs, peer, flat).start()

    low_recv[pl.ds(flat, 1)] = low_send[...][None]
    req_start(att_send, att_recv, att_ss, att_rs)
    att_recv[pl.ds(me, 1)] = att_send[pl.ds(me, 1)]
    square = jnp.concatenate(
        [summed[:, half:], jnp.zeros((128 - ROWS, 128), f32)], axis=0
    )
    flipped = jnp.transpose(square)
    maps_t[...] = flipped[: 2 * STATE] + flipped[2 * STATE : 4 * STATE]
    loads[8].wait()
    loads[9].wait()

    @pl.loop(1, total)
    def _(k):
        peer = lax.rem(flat + k, total)
        all_copy(low_send, low_recv, low_ss, low_rs, peer, peer).wait_recv()

    z = jnp.dot(low_recv[:n].reshape(rows, half), dtw[:half], preferred_element_type=f32)
    z = z + jnp.dot(low_recv[n:].reshape(rows, half), dtw[half:], preferred_element_type=f32)
    zbuf[...] = (z + dt_bias[:, here]).reshape(n, ROWS, cols)

    @pl.loop(0, n)
    def _(k):
        peer = lax.rem(me + 1 + k, n)
        block = zbuf[pl.ds(peer, 1)]
        delta = jnp.maximum(block, 0.0) + jnp.log1p(jnp.exp(-jnp.abs(block)))
        del_send[pl.ds(peer, 1)] = delta.astype(bf16)

        @pl.when(k < n - 1)
        def _():
            req_copy(del_send, del_recv, del_ss, del_rs, peer, me).start()

    del_recv[pl.ds(me, 1)] = del_send[pl.ds(me, 1)]
    for load in loads[10:13]:
        load.wait()
    req_wait(tok_send, tok_recv, tok_ss, tok_rs)

    @pl.loop(0, n)
    def _(k):
        peer = lax.rem(me - k + n, n)

        @pl.when(k > 0)
        def _():
            req_copy(del_send, del_recv, del_ss, del_rs, peer, peer).wait_recv()

        block = pl.ds(pl.multiple_of(peer * cols, cols), cols)
        delta = del_recv[peer].astype(f32)
        toks = tok_recv[peer].astype(f32)
        w2 = taps[2:3, block]
        w3 = taps[3:4, block]
        skip = skip_gain[:, block]
        x0 = pre[0:8, block] + toks[0:8] * w3
        x1 = pre[8:16, block] + toks[0:8] * w2 + toks[8:16] * w3
        x = jnp.concatenate([jax.nn.silu(x0), jax.nn.silu(x1)], axis=0)
        x = x.astype(bf16).astype(f32)
        dx = delta * x
        rate = -jnp.exp(decay[:, block])
        for s in range(slots):
            h = state[s, :, block]
            for t in range(STEPS):
                i = t * slots + s
                h = jnp.exp(delta[i : i + 1] * rate) * h + dx[i : i + 1] * maps_t[:STATE, i : i + 1]
                vbuf[i : i + 1, :] = jnp.sum(
                    h * maps_t[STATE:, i : i + 1], axis=0, keepdims=True
                )
        val_send[peer] = (vbuf[...] + skip * x).astype(bf16)

        @pl.when(k > 0)
        def _():
            req_copy(val_send, val_recv, val_ss, val_rs, peer, me).start()

    val_recv[pl.ds(me, 1)] = val_send[pl.ds(me, 1)]

    loads[13].wait()
    gate = jax.nn.silu(gate_in[...].reshape(rows, cols).astype(f32))
    req_wait(att_send, att_recv, att_ss, att_rs)
    att = jnp.dot(back, att_recv[...].reshape(rows, acols), preferred_element_type=f32)
    att_ref[...] = att.astype(bf16).reshape(att_ref.shape)
    req_wait(val_send, val_recv, val_ss, val_rs)
    val = jnp.dot(back, val_recv[...].reshape(rows, cols), preferred_element_type=f32)
    mamba_ref[...] = (val * gate).astype(bf16).reshape(mamba_ref.shape)

    req_drain(pre_send, pre_recv, pre_ss, pre_rs)
    req_drain(tok_send, tok_recv, tok_ss, tok_rs)
    req_drain(att_send, att_recv, att_ss, att_rs)
    req_drain(del_send, del_recv, del_ss, del_rs)
    req_drain(val_send, val_recv, val_ss, val_rs)

    @pl.loop(1, total)
    def _(k):
        peer = lax.rem(flat + k, total)
        all_copy(part_send.at[peer], part_recv, part_ss, part_rs, peer, flat).wait_send()
        all_copy(low_send, low_recv, low_ss, low_rs, peer, flat).wait_send()


def local_kernel(
    ssm_state,
    conv_state,
    token_input,
    gate_input,
    conv_weight,
    conv_bias,
    proj_weight,
    dt_weight,
    dt_bias,
    decay_log,
    skip_gain,
    queries,
    kv_pages,
    new_kv,
    page_table,
    context_len,
    decode_row,
):
    n = lax.axis_size("req")
    slots = ssm_state.shape[0]
    width = ssm_state.shape[2]
    total = decode_row.shape[0]
    cols = token_input.shape[2]
    acols = queries.shape[2] // n
    kv_heads = KVH // lax.axis_size("tp")
    pages, page = kv_pages.shape[1:3]
    rows = total * STEPS
    kv = kv_pages.reshape(2, pages * page, -1)
    half = DT_RANK // 2
    bf16, f32 = jnp.bfloat16, jnp.float32
    vmem = pl.BlockSpec(memory_space=pltpu.VMEM)
    hbm = pl.BlockSpec(memory_space=pl.ANY)
    dma = pltpu.SemaphoreType.DMA
    mamba, attended = pl.pallas_call(
        functools.partial(block_kernel, n, slots, cols, acols, kv_heads),
        out_shape=(
            jax.ShapeDtypeStruct((total, STEPS, cols), bf16),
            jax.ShapeDtypeStruct((total, STEPS, acols), bf16),
        ),
        in_specs=[hbm] * 14 + [vmem] * 3,
        out_specs=(vmem, vmem),
        scratch_shapes=[
            pltpu.VMEM(kv.shape, bf16),
            pltpu.VMEM(queries.shape, bf16),
            pltpu.VMEM(new_kv.shape, bf16),
            pltpu.VMEM(proj_weight.shape[::-1], bf16),
            pltpu.VMEM(dt_weight.shape, bf16),
            pltpu.VMEM(ssm_state.shape, f32),
            pltpu.VMEM(decay_log.shape, f32),
            pltpu.VMEM(gate_input.shape, bf16),
            pltpu.VMEM((1, width), f32),
            pltpu.VMEM((1, width), f32),
            pltpu.VMEM((CONV - 1, slots, width), f32),
            pltpu.VMEM(conv_weight.shape, f32),
            pltpu.VMEM((1, width), f32),
            pltpu.VMEM(token_input.shape, bf16),
            pltpu.VMEM((ROWS, width), f32),
            pltpu.VMEM((ROWS, pages * page), f32),
            pltpu.VMEM((ROWS, queries.shape[2]), bf16),
            pltpu.VMEM((2, ROWS, new_kv.shape[3]), bf16),
            pltpu.VMEM((n, ROWS, cols), bf16),
            pltpu.VMEM((n, ROWS, cols), bf16),
            pltpu.VMEM((n, ROWS, cols), bf16),
            pltpu.VMEM((n, ROWS, cols), bf16),
            pltpu.VMEM((2 * n, ROWS, half + 128), bf16),
            pltpu.VMEM((2 * n, ROWS, half + 128), bf16),
            pltpu.VMEM((ROWS, half), bf16),
            pltpu.VMEM((2 * n, ROWS, half), bf16),
            pltpu.VMEM((n, ROWS, cols), bf16),
            pltpu.VMEM((n, ROWS, cols), bf16),
            pltpu.VMEM((n, ROWS, cols), bf16),
            pltpu.VMEM((n, ROWS, cols), bf16),
            pltpu.VMEM((n, ROWS, acols), bf16),
            pltpu.VMEM((n, ROWS, acols), bf16),
            pltpu.VMEM((n, ROWS, cols), f32),
            pltpu.VMEM((ROWS, cols), f32),
            pltpu.VMEM((2 * STATE, 128), f32),
            dma((14,)),
            dma((n,)),
            dma((n,)),
            dma((n,)),
            dma((n,)),
            dma((2 * n,)),
            dma((2 * n,)),
            dma((2 * n,)),
            dma((2 * n,)),
            dma((n,)),
            dma((n,)),
            dma((n,)),
            dma((n,)),
            dma((n,)),
            dma((n,)),
        ],
        compiler_params=pltpu.CompilerParams(
            collective_id=0, has_side_effects=True, vmem_limit_bytes=60 * 2**20
        ),
    )(
        kv,
        queries,
        new_kv,
        proj_weight.T,
        dt_weight,
        ssm_state,
        decay_log,
        gate_input,
        dt_bias[None],
        skip_gain[None],
        conv_state.transpose(1, 0, 2),
        conv_weight,
        conv_bias[None],
        token_input,
        decode_row[None],
        page_table,
        context_len[None],
    )
    return mamba, attended


def solution(mesh):
    in_specs = (
        P(("groups", "req"), None, "tp"),
        P(("groups", "req"), None, "tp"),
        P("groups", None, ("tp", "req")),
        P("groups", None, ("tp", "req")),
        P(None, "tp"),
        P("tp"),
        P(("tp", "req"), None),
        P(None, ("tp", "req")),
        P("tp"),
        P(None, "tp"),
        P("tp"),
        P(("groups", "req"), None, "tp"),
        P(None, ("groups", "req"), None, "tp"),
        P(("groups", "req"), None, None, "tp"),
        P(("groups", "req"), None),
        P(("groups", "req")),
        P("groups"),
    )
    out_specs = (P("groups", None, ("tp", "req")), P("groups", None, ("tp", "req")))
    kernel_fits = mesh.shape["req"] <= 8 and mesh.shape["tp"] == 2
    body = local_kernel if kernel_fits else local
    return jax.shard_map(body, mesh=mesh, in_specs=in_specs, out_specs=out_specs, check_vma=False)
```

```python
import functools
import math

import jax
import jax.numpy as jnp
from jax import lax
from jax.experimental import pallas as pl
from jax.experimental.pallas import tpu as pltpu
from jax.sharding import PartitionSpec as P

STATE = 16
CONV = 4
DT_RANK = 512
HQ = 64
KVH = 8
HD = 128
STEPS = 2


def convolve(convs, tokens, conv_weight, conv_bias):
    window = jnp.concatenate([convs, tokens.astype(jnp.float32)], axis=1)
    results = []
    for step in range(STEPS):
        pre = conv_bias + window[:, step] * conv_weight[0]
        for tap in range(1, CONV):
            pre = pre + window[:, step + tap] * conv_weight[tap]
        results.append(jax.nn.silu(pre).astype(jnp.bfloat16))
    return jnp.stack(results, axis=1)


def project(mixed, proj_weight):
    partial_sum = jnp.einsum("rtc,cx->rtx", mixed, proj_weight, preferred_element_type=jnp.float32)
    return lax.psum(partial_sum, ("req", "tp"))


def step_sizes(proj, dt_weight, bias_cols):
    low = proj[:, :, :DT_RANK].astype(jnp.bfloat16)
    return jax.nn.softplus(
        jnp.einsum("rtk,kc->rtc", low, dt_weight, preferred_element_type=jnp.float32) + bias_cols
    )


def advance(hidden, mixed, delta, proj, gates, decay_log, skip_gain):
    rate = -jnp.exp(decay_log)
    results = []
    for step in range(STEPS):
        in_map = proj[:, step, DT_RANK : DT_RANK + STATE]
        out_map = proj[:, step, DT_RANK + STATE :]
        inputf = lax.optimization_barrier(mixed[:, step]).astype(jnp.float32)
        rates_now = delta[:, step]
        hidden = (
            jnp.exp(rates_now[:, None, :] * rate[None]) * hidden
            + rates_now[:, None, :] * in_map[:, :, None] * inputf[:, None, :]
        )
        value = jnp.sum(out_map[:, :, None] * hidden, axis=1) + skip_gain * inputf
        results.append(
            (value * jax.nn.silu(gates[:, step].astype(jnp.float32))).astype(jnp.bfloat16)
        )
    return jnp.stack(results, axis=1)


def attend(query, key_cache, value_cache, fresh, lens, heads, kv_heads):
    rows = query.shape[0]
    group = heads // kv_heads
    scale = 1.0 / math.sqrt(HD)
    queryq = query.reshape(rows, STEPS, kv_heads, group, HD)
    keys = key_cache.reshape(rows, -1, kv_heads, HD)
    values = value_cache.reshape(rows, -1, kv_heads, HD)
    new_keys = fresh[:, :, 0].reshape(rows, STEPS, kv_heads, HD)
    new_values = fresh[:, :, 1].reshape(rows, STEPS, kv_heads, HD)
    old = jnp.einsum("btkgd,bnkd->btkgn", queryq, keys, preferred_element_type=jnp.float32) * scale
    new = (
        jnp.einsum("btkgd,bskd->btkgs", queryq, new_keys, preferred_element_type=jnp.float32)
        * scale
    )
    live = jnp.arange(keys.shape[1])[None, :] < lens[:, None]
    causal = jnp.arange(STEPS)[None, :] <= jnp.arange(STEPS)[:, None]
    old = jnp.where(live[:, None, None, None, :], old, -1e30)
    new = jnp.where(causal[None, :, None, None, :], new, -1e30)
    top = jnp.maximum(jnp.max(old, axis=-1, keepdims=True), jnp.max(new, axis=-1, keepdims=True))
    exp_old = jnp.exp(old - top)
    exp_new = jnp.exp(new - top)
    total = jnp.sum(exp_old, axis=-1, keepdims=True) + jnp.sum(exp_new, axis=-1, keepdims=True)
    w_old = (exp_old / total).astype(jnp.bfloat16)
    w_new = (exp_new / total).astype(jnp.bfloat16)
    out = jnp.einsum("btkgn,bnkd->btkgd", w_old, values, preferred_element_type=jnp.float32)
    out = out + jnp.einsum(
        "btkgs,bskd->btkgd", w_new, new_values, preferred_element_type=jnp.float32
    )
    return out.reshape(rows, STEPS, heads * HD).astype(jnp.bfloat16)


def local(
    ssm_state,
    conv_state,
    token_input,
    gate_input,
    conv_weight,
    conv_bias,
    proj_weight,
    dt_weight,
    dt_bias,
    decay_log,
    skip_gain,
    queries,
    kv_pages,
    new_kv,
    page_table,
    context_len,
    decode_row,
):
    slots = ssm_state.shape[0]
    total = decode_row.shape[0]
    cols = token_input.shape[2]
    source = jnp.zeros((total,), jnp.int32).at[decode_row].set(jnp.arange(total, dtype=jnp.int32))
    offset = lax.axis_index("req") * cols
    heads = HQ // lax.axis_size("tp")
    kv_heads = KVH // lax.axis_size("tp")
    flat_pages = page_table.reshape(-1)
    key_cache = kv_pages[0][flat_pages].reshape(slots, -1, kv_heads * HD)
    value_cache = kv_pages[1][flat_pages].reshape(slots, -1, kv_heads * HD)
    attended = attend(queries, key_cache, value_cache, new_kv, context_len, heads, kv_heads)
    spread = lax.all_to_all(attended, "req", split_axis=2, concat_axis=0, tiled=True)
    attention_out = spread[source]
    bias_cols = lax.dynamic_slice_in_dim(dt_bias, offset, cols, 0)
    tok_slot, gate_slot = (
        lax.all_to_all(token_input[decode_row], "req", split_axis=0, concat_axis=2, tiled=True),
        lax.all_to_all(gate_input[decode_row], "req", split_axis=0, concat_axis=2, tiled=True),
    )
    mixed_slot = convolve(conv_state, tok_slot, conv_weight, conv_bias)
    mixed_cols = lax.all_to_all(mixed_slot, "req", split_axis=2, concat_axis=0, tiled=True)
    proj = project(mixed_cols, proj_weight)
    delta_cols = step_sizes(proj, dt_weight, bias_cols)
    delta = lax.all_to_all(delta_cols, "req", split_axis=0, concat_axis=2, tiled=True)
    mine = lax.dynamic_slice_in_dim(proj, lax.axis_index("req") * slots, slots, 0)
    result = advance(ssm_state, mixed_slot, delta, mine, gate_slot, decay_log, skip_gain)
    back = lax.all_to_all(result, "req", split_axis=2, concat_axis=0, tiled=True)
    mamba_out = back[source]
    return (mamba_out, attention_out)


ROWS = 16


def block_kernel(
    n,
    slots,
    cols,
    acols,
    kv_heads,
    kv_hbm,
    query_hbm,
    fresh_hbm,
    pw_hbm,
    dtw_hbm,
    state_hbm,
    decay_hbm,
    gate_hbm,
    dt_bias_hbm,
    skip_hbm,
    conv_hbm,
    taps_hbm,
    conv_bias_hbm,
    tok_hbm,
    row_ref,
    table_ref,
    len_ref,
    mamba_ref,
    att_ref,
    kv,
    query_in,
    fresh_in,
    pw,
    dtw,
    state,
    decay,
    gate_in,
    dt_bias,
    skip_gain,
    conv,
    taps,
    conv_bias,
    tok_in,
    pre,
    bias,
    query,
    fresh_ref,
    pre_send,
    pre_recv,
    tok_send,
    tok_recv,
    part_send,
    part_recv,
    low_send,
    low_recv,
    del_send,
    del_recv,
    val_send,
    val_recv,
    att_send,
    att_recv,
    zbuf,
    vbuf,
    maps_t,
    load_sem,
    pre_ss,
    pre_rs,
    tok_ss,
    tok_rs,
    part_ss,
    part_rs,
    low_ss,
    low_rs,
    del_ss,
    del_rs,
    val_ss,
    val_rs,
    att_ss,
    att_rs,
):
    me = lax.axis_index("req")
    core = lax.axis_index("tp")
    total = 2 * n
    flat = core * n + me
    rows = n * ROWS
    f32, bf16 = jnp.float32, jnp.bfloat16

    pairs = (
        (conv_hbm, conv),
        (taps_hbm, taps),
        (conv_bias_hbm, conv_bias),
        (tok_hbm, tok_in),
        (query_hbm, query_in),
        (fresh_hbm, fresh_in),
        (kv_hbm, kv),
        (pw_hbm, pw),
        (dt_bias_hbm, dt_bias),
        (dtw_hbm, dtw),
        (state_hbm, state),
        (decay_hbm, decay),
        (skip_hbm, skip_gain),
        (gate_hbm, gate_in),
    )
    loads = [
        pltpu.make_async_copy(src, dst, load_sem.at[i]) for i, (src, dst) in enumerate(pairs)
    ]
    for load in loads:
        load.start()

    barrier = pltpu.get_barrier_semaphore()

    @pl.loop(1, total)
    def _(k):
        other = lax.rem(flat + k, total)
        pl.semaphore_signal(
            barrier,
            inc=1,
            device_id={"req": lax.rem(other, n), "tp": other // n},
            device_id_type=pl.DeviceIdType.MESH,
        )

    def req_copy(src, dst, ss, rs, peer, slot):
        return pltpu.make_async_remote_copy(
            src_ref=src.at[peer],
            dst_ref=dst.at[slot],
            send_sem=ss.at[peer],
            recv_sem=rs.at[slot],
            device_id={"req": peer, "tp": core},
            device_id_type=pl.DeviceIdType.MESH,
        )

    def req_start(src, dst, ss, rs):
        @pl.loop(1, n)
        def _(k):
            peer = lax.rem(me + k, n)
            req_copy(src, dst, ss, rs, peer, me).start()

    def req_wait(src, dst, ss, rs):
        @pl.loop(1, n)
        def _(k):
            peer = lax.rem(me + k, n)
            req_copy(src, dst, ss, rs, peer, peer).wait_recv()

    def req_drain(src, dst, ss, rs):
        @pl.loop(1, n)
        def _(k):
            peer = lax.rem(me + k, n)
            req_copy(src, dst, ss, rs, peer, me).wait_send()

    def all_copy(src, dst, ss, rs, peer, slot):
        return pltpu.make_async_remote_copy(
            src_ref=src,
            dst_ref=dst.at[slot],
            send_sem=ss.at[peer],
            recv_sem=rs.at[slot],
            device_id={"req": lax.rem(peer, n), "tp": peer // n},
            device_id_type=pl.DeviceIdType.MESH,
        )

    for load in loads[:3]:
        load.wait()

    @pl.loop(0, n)
    def _(j):
        block = pl.ds(pl.multiple_of(j * cols, cols), cols)
        w = [taps[i : i + 1, block] for i in range(CONV)]
        oldest, older, last = conv[0, :, block], conv[1, :, block], conv[2, :, block]
        base = conv_bias[:, block]
        first = base + oldest * w[0] + older * w[1] + last * w[2]
        second = base + older * w[0] + last * w[1]
        both = jnp.concatenate([first, second], axis=0)
        pre[:, block] = both
        pre_send[pl.ds(j, 1)] = both.astype(bf16)[None]

    def iota(shape, axis):
        return lax.broadcasted_iota(jnp.int32, shape, axis)

    def hot(condition):
        return jnp.where(condition, 1.0, 0.0).astype(bf16)

    requests = n * slots
    where_row = hot(row_ref[...] == iota((rows, requests), 0) // STEPS)
    column = iota((requests, rows), 1)
    slot_of = column // ROWS * slots + column % slots
    spread = hot(slot_of == iota((requests, rows), 0))
    same_step = iota((rows, rows), 1) % ROWS // slots == iota((rows, rows), 0) % STEPS
    back = jnp.dot(where_row, spread, preferred_element_type=f32)
    back = jnp.where(same_step, back, 0.0).astype(bf16)
    loads[3].wait()
    tok = lax.dot_general(
        back,
        tok_in[...].reshape(rows, cols),
        (((0,), (0,)), ((), ())),
        preferred_element_type=f32,
    )
    tok_send[...] = tok.astype(bf16).reshape(n, ROWS, cols)

    pl.semaphore_wait(barrier, total - 1)
    req_start(pre_send, pre_recv, pre_ss, pre_rs)
    pre_recv[pl.ds(me, 1)] = pre_send[pl.ds(me, 1)]
    tok_recv[pl.ds(me, 1)] = tok_send[pl.ds(me, 1)]

    pages = table_ref.shape[1]
    page = kv.shape[1] // pages
    per_slot = pages // slots
    lens = jnp.sum(
        jnp.where(
            iota((slots, slots), 0) == iota((slots, slots), 1), len_ref[...].astype(f32), 0.0
        ),
        axis=1,
        keepdims=True,
    )
    entry = iota((slots, pages), 1)
    counts = lens - (entry % per_slot * page).astype(f32)
    counts = jnp.where(
        entry // per_slot == iota((slots, pages), 0), jnp.clip(counts, 0.0, float(page)), 0.0
    )
    held = hot(table_ref[...] == iota((pages, pages), 0))
    counts = lax.dot_general(
        counts.astype(bf16), held, (((1,), (1,)), ((), ())), preferred_element_type=f32
    )
    widen = hot(iota((pages, pages * page), 1) // page == iota((pages, pages * page), 0))
    counts = jnp.dot(counts.astype(bf16), widen, preferred_element_type=f32)
    token = (iota((slots, pages * page), 1) % page).astype(f32)
    live = jnp.where(token < counts, 0.0, -1e30)
    bias[...] = jnp.concatenate([live] * STEPS, axis=0)
    turned = (iota((ROWS, ROWS), 0) % slots) * STEPS + iota((ROWS, ROWS), 0) // slots
    turn = hot(turned == iota((ROWS, ROWS), 1))
    for load in loads[4:7]:
        load.wait()
    query[...] = jnp.dot(
        turn, query_in[...].reshape(ROWS, -1), preferred_element_type=f32
    ).astype(bf16)
    row32, col32 = iota((2 * ROWS, 2 * ROWS), 0), iota((2 * ROWS, 2 * ROWS), 1)
    pick = (row32 % slots) * 2 * STEPS + (row32 % ROWS) // slots * 2 + row32 // ROWS
    fresh = jnp.dot(
        hot(pick == col32),
        fresh_in[...].reshape(2 * ROWS, -1),
        preferred_element_type=f32,
    ).astype(bf16)
    row16, col16 = iota((ROWS, ROWS), 0), iota((ROWS, ROWS), 1)
    allowed = (row16 % slots == col16 % slots) & (col16 // slots <= row16 // slots)
    fresh_bias = jnp.where(allowed, 0.0, -1e30)
    fresh_ref[...] = fresh.reshape(2, ROWS, -1)
    group = (acols * n) // (kv_heads * HD)
    per_block = acols // HD
    scale = 1.0 / math.sqrt(HD)
    contract = (((1,), (1,)), ((), ()))

    def attend_head(h):
        lanes = pl.ds(pl.multiple_of(h * HD, HD), HD)
        q = jnp.concatenate(
            [
                query[:, pl.ds(pl.multiple_of((h * group + g) * HD, HD), HD)]
                for g in range(group)
            ],
            axis=0,
        )
        old = lax.dot_general(q, kv[0, :, lanes], contract, preferred_element_type=f32)
        new = lax.dot_general(
            q, fresh_ref[0, :, lanes], contract, preferred_element_type=f32
        )
        old = old.reshape(group, ROWS, -1) * scale + bias[...][None]
        new = new.reshape(group, ROWS, -1) * scale + fresh_bias[None]
        top = jnp.maximum(
            jnp.max(old, axis=-1, keepdims=True), jnp.max(new, axis=-1, keepdims=True)
        )
        old = jnp.exp(old - top)
        new = jnp.exp(new - top)
        norm = jnp.sum(old, axis=-1, keepdims=True) + jnp.sum(new, axis=-1, keepdims=True)
        old = old.astype(bf16).reshape(group * ROWS, -1)
        new = new.astype(bf16).reshape(group * ROWS, -1)
        out = jnp.dot(old, kv[1, :, lanes], preferred_element_type=f32)
        out = out + jnp.dot(new, fresh_ref[1, :, lanes], preferred_element_type=f32)
        out = (out.reshape(group, ROWS, HD) / norm).astype(bf16)
        for g in range(group):
            place = g % per_block
            att_send[h * (group // per_block) + g // per_block, :, place * HD : (place + 1) * HD] = out[g]

    early = kv_heads // 2
    pl.loop(0, early)(attend_head)

    here = pl.ds(pl.multiple_of(me * cols, cols), cols)
    w2, w3 = taps[2:3, here], taps[3:4, here]
    tok4 = tok.reshape(n, 2, 8, cols)
    req_wait(pre_send, pre_recv, pre_ss, pre_rs)
    req_start(tok_send, tok_recv, tok_ss, tok_rs)
    pre4 = pre_recv[...].astype(f32).reshape(n, 2, 8, cols)
    first = pre4[:, 0] + tok4[:, 0] * w3[None]
    second = pre4[:, 1] + tok4[:, 0] * w2[None] + tok4[:, 1] * w3[None]
    mixed = jnp.stack([jax.nn.silu(first), jax.nn.silu(second)], axis=1)
    mixed = mixed.reshape(rows, cols).astype(bf16)
    loads[7].wait()
    part = lax.dot_general(mixed, pw[...], contract, preferred_element_type=f32)
    half = DT_RANK // 2
    maps = part[:, DT_RANK:]
    upper = maps.astype(bf16).astype(f32)
    maps = jnp.concatenate(
        [upper, maps - upper, jnp.zeros((rows, 128 - 4 * STATE), f32)], axis=1
    )
    for c in range(2):
        part_send[c * n : (c + 1) * n, :, :half] = (
            part[:, c * half : (c + 1) * half].astype(bf16).reshape(n, ROWS, half)
        )
        part_send[c * n : (c + 1) * n, :, half:] = maps.astype(bf16).reshape(n, ROWS, 128)

    @pl.loop(1, total)
    def _(k):
        peer = lax.rem(flat + k, total)
        all_copy(part_send.at[peer], part_recv, part_ss, part_rs, peer, flat).start()

    part_recv[pl.ds(flat, 1)] = part_send[pl.ds(flat, 1)]
    pl.loop(early, kv_heads)(attend_head)

    @pl.loop(1, total)
    def _(k):
        peer = lax.rem(flat + k, total)
        all_copy(part_send.at[peer], part_recv, part_ss, part_rs, peer, peer).wait_recv()

    summed = jnp.sum(part_recv[...].astype(f32), axis=0)
    low_send[...] = summed[:, :half].astype(bf16)

    @pl.loop(1, total)
    def _(k):
        peer = lax.rem(flat + k, total)
        all_copy(low_send, low_recv, low_ss, low_rs, peer, flat).start()

    low_recv[pl.ds(flat, 1)] = low_send[...][None]
    req_start(att_send, att_recv, att_ss, att_rs)
    att_recv[pl.ds(me, 1)] = att_send[pl.ds(me, 1)]
    square = jnp.concatenate(
        [summed[:, half:], jnp.zeros((128 - ROWS, 128), f32)], axis=0
    )
    flipped = jnp.transpose(square)
    maps_t[...] = flipped[: 2 * STATE] + flipped[2 * STATE : 4 * STATE]
    loads[8].wait()
    loads[9].wait()

    @pl.loop(1, total)
    def _(k):
        peer = lax.rem(flat + k, total)
        all_copy(low_send, low_recv, low_ss, low_rs, peer, peer).wait_recv()

    z = jnp.dot(low_recv[:n].reshape(rows, half), dtw[:half], preferred_element_type=f32)
    z = z + jnp.dot(low_recv[n:].reshape(rows, half), dtw[half:], preferred_element_type=f32)
    zbuf[...] = (z + dt_bias[:, here]).reshape(n, ROWS, cols)

    @pl.loop(0, n)
    def _(k):
        peer = lax.rem(me + 1 + k, n)
        block = zbuf[pl.ds(peer, 1)]
        delta = jnp.maximum(block, 0.0) + jnp.log1p(jnp.exp(-jnp.abs(block)))
        del_send[pl.ds(peer, 1)] = delta.astype(bf16)

        @pl.when(k < n - 1)
        def _():
            req_copy(del_send, del_recv, del_ss, del_rs, peer, me).start()

    del_recv[pl.ds(me, 1)] = del_send[pl.ds(me, 1)]
    for load in loads[10:13]:
        load.wait()
    req_wait(tok_send, tok_recv, tok_ss, tok_rs)

    @pl.loop(0, n)
    def _(k):
        peer = lax.rem(me - k + n, n)

        @pl.when(k > 0)
        def _():
            req_copy(del_send, del_recv, del_ss, del_rs, peer, peer).wait_recv()

        block = pl.ds(pl.multiple_of(peer * cols, cols), cols)
        delta = del_recv[peer].astype(f32)
        toks = tok_recv[peer].astype(f32)
        w2 = taps[2:3, block]
        w3 = taps[3:4, block]
        skip = skip_gain[:, block]
        x0 = pre[0:8, block] + toks[0:8] * w3
        x1 = pre[8:16, block] + toks[0:8] * w2 + toks[8:16] * w3
        x = jnp.concatenate([jax.nn.silu(x0), jax.nn.silu(x1)], axis=0)
        x = x.astype(bf16).astype(f32)
        dx = delta * x
        rate = -jnp.exp(decay[:, block])
        for s in range(slots):
            h = state[s, :, block]
            for t in range(STEPS):
                i = t * slots + s
                h = jnp.exp(delta[i : i + 1] * rate) * h + dx[i : i + 1] * maps_t[:STATE, i : i + 1]
                vbuf[i : i + 1, :] = jnp.sum(
                    h * maps_t[STATE:, i : i + 1], axis=0, keepdims=True
                )
        val_send[peer] = (vbuf[...] + skip * x).astype(bf16)

        @pl.when(k > 0)
        def _():
            req_copy(val_send, val_recv, val_ss, val_rs, peer, me).start()

    val_recv[pl.ds(me, 1)] = val_send[pl.ds(me, 1)]

    loads[13].wait()
    gate = jax.nn.silu(gate_in[...].reshape(rows, cols).astype(f32))
    req_wait(att_send, att_recv, att_ss, att_rs)
    att = jnp.dot(back, att_recv[...].reshape(rows, acols), preferred_element_type=f32)
    att_ref[...] = att.astype(bf16).reshape(att_ref.shape)
    req_wait(val_send, val_recv, val_ss, val_rs)
    val = jnp.dot(back, val_recv[...].reshape(rows, cols), preferred_element_type=f32)
    mamba_ref[...] = (val * gate).astype(bf16).reshape(mamba_ref.shape)

    req_drain(pre_send, pre_recv, pre_ss, pre_rs)
    req_drain(tok_send, tok_recv, tok_ss, tok_rs)
    req_drain(att_send, att_recv, att_ss, att_rs)
    req_drain(del_send, del_recv, del_ss, del_rs)
    req_drain(val_send, val_recv, val_ss, val_rs)

    @pl.loop(1, total)
    def _(k):
        peer = lax.rem(flat + k, total)
        all_copy(part_send.at[peer], part_recv, part_ss, part_rs, peer, flat).wait_send()
        all_copy(low_send, low_recv, low_ss, low_rs, peer, flat).wait_send()


def place_kernel(mamba_in, att_in, mamba_out, att_out, sem):
    first = pltpu.make_async_copy(mamba_in, mamba_out, sem.at[0])
    second = pltpu.make_async_copy(att_in, att_out, sem.at[1])
    first.start()
    second.start()
    first.wait()
    second.wait()


def local_kernel(
    ssm_state,
    conv_state,
    token_input,
    gate_input,
    conv_weight,
    conv_bias,
    proj_weight,
    dt_weight,
    dt_bias,
    decay_log,
    skip_gain,
    queries,
    kv_pages,
    new_kv,
    page_table,
    context_len,
    decode_row,
):
    n = lax.axis_size("req")
    slots = ssm_state.shape[0]
    width = ssm_state.shape[2]
    total = decode_row.shape[0]
    cols = token_input.shape[2]
    acols = queries.shape[2] // n
    kv_heads = KVH // lax.axis_size("tp")
    pages, page = kv_pages.shape[1:3]
    rows = total * STEPS
    kv = kv_pages.reshape(2, pages * page, -1)
    half = DT_RANK // 2
    bf16, f32 = jnp.bfloat16, jnp.float32
    vmem = pl.BlockSpec(memory_space=pltpu.VMEM)
    hbm = pl.BlockSpec(memory_space=pl.ANY)
    dma = pltpu.SemaphoreType.DMA
    mamba, attended = pl.pallas_call(
        functools.partial(block_kernel, n, slots, cols, acols, kv_heads),
        out_shape=(
            jax.ShapeDtypeStruct((total, STEPS, cols), bf16),
            jax.ShapeDtypeStruct((total, STEPS, acols), bf16),
        ),
        in_specs=[hbm] * 14 + [vmem] * 3,
        out_specs=(vmem, vmem),
        scratch_shapes=[
            pltpu.VMEM(kv.shape, bf16),
            pltpu.VMEM(queries.shape, bf16),
            pltpu.VMEM(new_kv.shape, bf16),
            pltpu.VMEM(proj_weight.shape[::-1], bf16),
            pltpu.VMEM(dt_weight.shape, bf16),
            pltpu.VMEM(ssm_state.shape, f32),
            pltpu.VMEM(decay_log.shape, f32),
            pltpu.VMEM(gate_input.shape, bf16),
            pltpu.VMEM((1, width), f32),
            pltpu.VMEM((1, width), f32),
            pltpu.VMEM((CONV - 1, slots, width), f32),
            pltpu.VMEM(conv_weight.shape, f32),
            pltpu.VMEM((1, width), f32),
            pltpu.VMEM(token_input.shape, bf16),
            pltpu.VMEM((ROWS, width), f32),
            pltpu.VMEM((ROWS, pages * page), f32),
            pltpu.VMEM((ROWS, queries.shape[2]), bf16),
            pltpu.VMEM((2, ROWS, new_kv.shape[3]), bf16),
            pltpu.VMEM((n, ROWS, cols), bf16),
            pltpu.VMEM((n, ROWS, cols), bf16),
            pltpu.VMEM((n, ROWS, cols), bf16),
            pltpu.VMEM((n, ROWS, cols), bf16),
            pltpu.VMEM((2 * n, ROWS, half + 128), bf16),
            pltpu.VMEM((2 * n, ROWS, half + 128), bf16),
            pltpu.VMEM((ROWS, half), bf16),
            pltpu.VMEM((2 * n, ROWS, half), bf16),
            pltpu.VMEM((n, ROWS, cols), bf16),
            pltpu.VMEM((n, ROWS, cols), bf16),
            pltpu.VMEM((n, ROWS, cols), bf16),
            pltpu.VMEM((n, ROWS, cols), bf16),
            pltpu.VMEM((n, ROWS, acols), bf16),
            pltpu.VMEM((n, ROWS, acols), bf16),
            pltpu.VMEM((n, ROWS, cols), f32),
            pltpu.VMEM((ROWS, cols), f32),
            pltpu.VMEM((2 * STATE, 128), f32),
            dma((14,)),
            dma((n,)),
            dma((n,)),
            dma((n,)),
            dma((n,)),
            dma((2 * n,)),
            dma((2 * n,)),
            dma((2 * n,)),
            dma((2 * n,)),
            dma((n,)),
            dma((n,)),
            dma((n,)),
            dma((n,)),
            dma((n,)),
            dma((n,)),
        ],
        compiler_params=pltpu.CompilerParams(
            collective_id=0, has_side_effects=True, vmem_limit_bytes=60 * 2**20
        ),
    )(
        kv,
        queries,
        new_kv,
        proj_weight.T,
        dt_weight,
        ssm_state,
        decay_log,
        gate_input,
        dt_bias[None],
        skip_gain[None],
        conv_state.transpose(1, 0, 2),
        conv_weight,
        conv_bias[None],
        token_input,
        decode_row[None],
        page_table,
        context_len[None],
    )
    return pl.pallas_call(
        place_kernel,
        out_shape=(
            jax.ShapeDtypeStruct(mamba.shape, bf16),
            jax.ShapeDtypeStruct(attended.shape, bf16),
        ),
        in_specs=[hbm] * 2,
        out_specs=(hbm, hbm),
        scratch_shapes=[dma((2,))],
        compiler_params=pltpu.CompilerParams(vmem_limit_bytes=60 * 2**20),
    )(mamba, attended)


def solution(mesh):
    in_specs = (
        P(("groups", "req"), None, "tp"),
        P(("groups", "req"), None, "tp"),
        P("groups", None, ("tp", "req")),
        P("groups", None, ("tp", "req")),
        P(None, "tp"),
        P("tp"),
        P(("tp", "req"), None),
        P(None, ("tp", "req")),
        P("tp"),
        P(None, "tp"),
        P("tp"),
        P(("groups", "req"), None, "tp"),
        P(None, ("groups", "req"), None, "tp"),
        P(("groups", "req"), None, None, "tp"),
        P(("groups", "req"), None),
        P(("groups", "req")),
        P("groups"),
    )
    out_specs = (P("groups", None, ("tp", "req")), P("groups", None, ("tp", "req")))
    kernel_fits = mesh.shape["req"] <= 8 and mesh.shape["tp"] == 2
    body = local_kernel if kernel_fits else local
    return jax.shard_map(body, mesh=mesh, in_specs=in_specs, out_specs=out_specs, check_vma=False)
```

```python
import functools
import math

import jax
import jax.numpy as jnp
from jax import lax
from jax.experimental import pallas as pl
from jax.experimental.pallas import tpu as pltpu
from jax.sharding import PartitionSpec as P

STATE = 16
CONV = 4
DT_RANK = 512
HQ = 64
KVH = 8
HD = 128
STEPS = 2


def convolve(convs, tokens, conv_weight, conv_bias):
    window = jnp.concatenate([convs, tokens.astype(jnp.float32)], axis=1)
    results = []
    for step in range(STEPS):
        pre = conv_bias + window[:, step] * conv_weight[0]
        for tap in range(1, CONV):
            pre = pre + window[:, step + tap] * conv_weight[tap]
        results.append(jax.nn.silu(pre).astype(jnp.bfloat16))
    return jnp.stack(results, axis=1)


def project(mixed, proj_weight):
    partial_sum = jnp.einsum("rtc,cx->rtx", mixed, proj_weight, preferred_element_type=jnp.float32)
    return lax.psum(partial_sum, ("req", "tp"))


def step_sizes(proj, dt_weight, bias_cols):
    low = proj[:, :, :DT_RANK].astype(jnp.bfloat16)
    return jax.nn.softplus(
        jnp.einsum("rtk,kc->rtc", low, dt_weight, preferred_element_type=jnp.float32) + bias_cols
    )


def advance(hidden, mixed, delta, proj, gates, decay_log, skip_gain):
    rate = -jnp.exp(decay_log)
    results = []
    for step in range(STEPS):
        in_map = proj[:, step, DT_RANK : DT_RANK + STATE]
        out_map = proj[:, step, DT_RANK + STATE :]
        inputf = lax.optimization_barrier(mixed[:, step]).astype(jnp.float32)
        rates_now = delta[:, step]
        hidden = (
            jnp.exp(rates_now[:, None, :] * rate[None]) * hidden
            + rates_now[:, None, :] * in_map[:, :, None] * inputf[:, None, :]
        )
        value = jnp.sum(out_map[:, :, None] * hidden, axis=1) + skip_gain * inputf
        results.append(
            (value * jax.nn.silu(gates[:, step].astype(jnp.float32))).astype(jnp.bfloat16)
        )
    return jnp.stack(results, axis=1)


def attend(query, key_cache, value_cache, fresh, lens, heads, kv_heads):
    rows = query.shape[0]
    group = heads // kv_heads
    scale = 1.0 / math.sqrt(HD)
    queryq = query.reshape(rows, STEPS, kv_heads, group, HD)
    keys = key_cache.reshape(rows, -1, kv_heads, HD)
    values = value_cache.reshape(rows, -1, kv_heads, HD)
    new_keys = fresh[:, :, 0].reshape(rows, STEPS, kv_heads, HD)
    new_values = fresh[:, :, 1].reshape(rows, STEPS, kv_heads, HD)
    old = jnp.einsum("btkgd,bnkd->btkgn", queryq, keys, preferred_element_type=jnp.float32) * scale
    new = (
        jnp.einsum("btkgd,bskd->btkgs", queryq, new_keys, preferred_element_type=jnp.float32)
        * scale
    )
    live = jnp.arange(keys.shape[1])[None, :] < lens[:, None]
    causal = jnp.arange(STEPS)[None, :] <= jnp.arange(STEPS)[:, None]
    old = jnp.where(live[:, None, None, None, :], old, -1e30)
    new = jnp.where(causal[None, :, None, None, :], new, -1e30)
    top = jnp.maximum(jnp.max(old, axis=-1, keepdims=True), jnp.max(new, axis=-1, keepdims=True))
    exp_old = jnp.exp(old - top)
    exp_new = jnp.exp(new - top)
    total = jnp.sum(exp_old, axis=-1, keepdims=True) + jnp.sum(exp_new, axis=-1, keepdims=True)
    w_old = (exp_old / total).astype(jnp.bfloat16)
    w_new = (exp_new / total).astype(jnp.bfloat16)
    out = jnp.einsum("btkgn,bnkd->btkgd", w_old, values, preferred_element_type=jnp.float32)
    out = out + jnp.einsum(
        "btkgs,bskd->btkgd", w_new, new_values, preferred_element_type=jnp.float32
    )
    return out.reshape(rows, STEPS, heads * HD).astype(jnp.bfloat16)


def local(
    ssm_state,
    conv_state,
    token_input,
    gate_input,
    conv_weight,
    conv_bias,
    proj_weight,
    dt_weight,
    dt_bias,
    decay_log,
    skip_gain,
    queries,
    kv_pages,
    new_kv,
    page_table,
    context_len,
    decode_row,
):
    slots = ssm_state.shape[0]
    total = decode_row.shape[0]
    cols = token_input.shape[2]
    source = jnp.zeros((total,), jnp.int32).at[decode_row].set(jnp.arange(total, dtype=jnp.int32))
    offset = lax.axis_index("req") * cols
    heads = HQ // lax.axis_size("tp")
    kv_heads = KVH // lax.axis_size("tp")
    flat_pages = page_table.reshape(-1)
    key_cache = kv_pages[0][flat_pages].reshape(slots, -1, kv_heads * HD)
    value_cache = kv_pages[1][flat_pages].reshape(slots, -1, kv_heads * HD)
    attended = attend(queries, key_cache, value_cache, new_kv, context_len, heads, kv_heads)
    spread = lax.all_to_all(attended, "req", split_axis=2, concat_axis=0, tiled=True)
    attention_out = spread[source]
    bias_cols = lax.dynamic_slice_in_dim(dt_bias, offset, cols, 0)
    tok_slot, gate_slot = (
        lax.all_to_all(token_input[decode_row], "req", split_axis=0, concat_axis=2, tiled=True),
        lax.all_to_all(gate_input[decode_row], "req", split_axis=0, concat_axis=2, tiled=True),
    )
    mixed_slot = convolve(conv_state, tok_slot, conv_weight, conv_bias)
    mixed_cols = lax.all_to_all(mixed_slot, "req", split_axis=2, concat_axis=0, tiled=True)
    proj = project(mixed_cols, proj_weight)
    delta_cols = step_sizes(proj, dt_weight, bias_cols)
    delta = lax.all_to_all(delta_cols, "req", split_axis=0, concat_axis=2, tiled=True)
    mine = lax.dynamic_slice_in_dim(proj, lax.axis_index("req") * slots, slots, 0)
    result = advance(ssm_state, mixed_slot, delta, mine, gate_slot, decay_log, skip_gain)
    back = lax.all_to_all(result, "req", split_axis=2, concat_axis=0, tiled=True)
    mamba_out = back[source]
    return (mamba_out, attention_out)


ROWS = 16


def block_kernel(
    n,
    slots,
    cols,
    acols,
    kv_heads,
    kv_hbm,
    query_hbm,
    fresh_hbm,
    pw_hbm,
    dtw_hbm,
    state_hbm,
    decay_hbm,
    gate_hbm,
    dt_bias_hbm,
    skip_hbm,
    conv_hbm,
    taps_hbm,
    conv_bias_hbm,
    tok_hbm,
    row_ref,
    table_ref,
    len_ref,
    mamba_ref,
    att_ref,
    kv,
    query_in,
    fresh_in,
    pw,
    dtw,
    state,
    decay,
    gate_in,
    dt_bias,
    skip_gain,
    conv,
    taps,
    conv_bias,
    tok_in,
    pre,
    bias,
    query,
    fresh_ref,
    pre_send,
    pre_recv,
    tok_send,
    tok_recv,
    part_send,
    part_recv,
    low_send,
    low_recv,
    del_send,
    del_recv,
    val_send,
    val_recv,
    att_send,
    att_recv,
    zbuf,
    vbuf,
    maps_t,
    load_sem,
    pre_ss,
    pre_rs,
    tok_ss,
    tok_rs,
    part_ss,
    part_rs,
    low_ss,
    low_rs,
    del_ss,
    del_rs,
    val_ss,
    val_rs,
    att_ss,
    att_rs,
):
    me = lax.axis_index("req")
    core = lax.axis_index("tp")
    total = 2 * n
    flat = core * n + me
    rows = n * ROWS
    f32, bf16 = jnp.float32, jnp.bfloat16

    pairs = (
        (conv_hbm, conv),
        (taps_hbm, taps),
        (conv_bias_hbm, conv_bias),
        (tok_hbm, tok_in),
        (query_hbm, query_in),
        (fresh_hbm, fresh_in),
        (kv_hbm, kv),
        (pw_hbm, pw),
        (dt_bias_hbm, dt_bias),
        (dtw_hbm, dtw),
        (state_hbm, state),
        (decay_hbm, decay),
        (skip_hbm, skip_gain),
        (gate_hbm, gate_in),
    )
    loads = [
        pltpu.make_async_copy(src, dst, load_sem.at[i]) for i, (src, dst) in enumerate(pairs)
    ]
    for load in loads:
        load.start()

    barrier = pltpu.get_barrier_semaphore()

    @pl.loop(1, total)
    def _(k):
        other = lax.rem(flat + k, total)
        pl.semaphore_signal(
            barrier,
            inc=1,
            device_id={"req": lax.rem(other, n), "tp": other // n},
            device_id_type=pl.DeviceIdType.MESH,
        )

    def req_copy(src, dst, ss, rs, peer, slot):
        return pltpu.make_async_remote_copy(
            src_ref=src.at[peer],
            dst_ref=dst.at[slot],
            send_sem=ss.at[peer],
            recv_sem=rs.at[slot],
            device_id={"req": peer, "tp": core},
            device_id_type=pl.DeviceIdType.MESH,
        )

    def req_start(src, dst, ss, rs):
        @pl.loop(1, n)
        def _(k):
            peer = lax.rem(me + k, n)
            req_copy(src, dst, ss, rs, peer, me).start()

    def req_wait(src, dst, ss, rs):
        @pl.loop(1, n)
        def _(k):
            peer = lax.rem(me + k, n)
            req_copy(src, dst, ss, rs, peer, peer).wait_recv()

    def req_drain(src, dst, ss, rs):
        @pl.loop(1, n)
        def _(k):
            peer = lax.rem(me + k, n)
            req_copy(src, dst, ss, rs, peer, me).wait_send()

    def all_copy(src, dst, ss, rs, peer, slot):
        return pltpu.make_async_remote_copy(
            src_ref=src,
            dst_ref=dst.at[slot],
            send_sem=ss.at[peer],
            recv_sem=rs.at[slot],
            device_id={"req": lax.rem(peer, n), "tp": peer // n},
            device_id_type=pl.DeviceIdType.MESH,
        )

    for load in loads[:3]:
        load.wait()

    @pl.loop(0, n)
    def _(j):
        block = pl.ds(pl.multiple_of(j * cols, cols), cols)
        w = [taps[i : i + 1, block] for i in range(CONV)]
        oldest, older, last = conv[0, :, block], conv[1, :, block], conv[2, :, block]
        base = conv_bias[:, block]
        first = base + oldest * w[0] + older * w[1] + last * w[2]
        second = base + older * w[0] + last * w[1]
        both = jnp.concatenate([first, second], axis=0)
        pre[:, block] = both
        pre_send[pl.ds(j, 1)] = both.astype(bf16)[None]

    def iota(shape, axis):
        return lax.broadcasted_iota(jnp.int32, shape, axis)

    def hot(condition):
        return jnp.where(condition, 1.0, 0.0).astype(bf16)

    requests = n * slots
    where_row = hot(row_ref[...] == iota((rows, requests), 0) // STEPS)
    column = iota((requests, rows), 1)
    slot_of = column // ROWS * slots + column % slots
    spread = hot(slot_of == iota((requests, rows), 0))
    same_step = iota((rows, rows), 1) % ROWS // slots == iota((rows, rows), 0) % STEPS
    back = jnp.dot(where_row, spread, preferred_element_type=f32)
    back = jnp.where(same_step, back, 0.0).astype(bf16)
    loads[3].wait()
    tok = lax.dot_general(
        back,
        tok_in[...].reshape(rows, cols),
        (((0,), (0,)), ((), ())),
        preferred_element_type=f32,
    )
    tok_send[...] = tok.astype(bf16).reshape(n, ROWS, cols)

    pl.semaphore_wait(barrier, total - 1)
    req_start(pre_send, pre_recv, pre_ss, pre_rs)
    pre_recv[pl.ds(me, 1)] = pre_send[pl.ds(me, 1)]
    tok_recv[pl.ds(me, 1)] = tok_send[pl.ds(me, 1)]

    pages = table_ref.shape[1]
    page = kv.shape[1] // pages
    per_slot = pages // slots
    lens = jnp.sum(
        jnp.where(
            iota((slots, slots), 0) == iota((slots, slots), 1), len_ref[...].astype(f32), 0.0
        ),
        axis=1,
        keepdims=True,
    )
    entry = iota((slots, pages), 1)
    counts = lens - (entry % per_slot * page).astype(f32)
    counts = jnp.where(
        entry // per_slot == iota((slots, pages), 0), jnp.clip(counts, 0.0, float(page)), 0.0
    )
    held = hot(table_ref[...] == iota((pages, pages), 0))
    counts = lax.dot_general(
        counts.astype(bf16), held, (((1,), (1,)), ((), ())), preferred_element_type=f32
    )
    widen = hot(iota((pages, pages * page), 1) // page == iota((pages, pages * page), 0))
    counts = jnp.dot(counts.astype(bf16), widen, preferred_element_type=f32)
    token = (iota((slots, pages * page), 1) % page).astype(f32)
    live = jnp.where(token < counts, 0.0, -1e30)
    bias[...] = jnp.concatenate([live] * STEPS, axis=0)
    turned = (iota((ROWS, ROWS), 0) % slots) * STEPS + iota((ROWS, ROWS), 0) // slots
    turn = hot(turned == iota((ROWS, ROWS), 1))
    for load in loads[4:7]:
        load.wait()
    query[...] = jnp.dot(
        turn, query_in[...].reshape(ROWS, -1), preferred_element_type=f32
    ).astype(bf16)
    row32, col32 = iota((2 * ROWS, 2 * ROWS), 0), iota((2 * ROWS, 2 * ROWS), 1)
    pick = (row32 % slots) * 2 * STEPS + (row32 % ROWS) // slots * 2 + row32 // ROWS
    fresh = jnp.dot(
        hot(pick == col32),
        fresh_in[...].reshape(2 * ROWS, -1),
        preferred_element_type=f32,
    ).astype(bf16)
    row16, col16 = iota((ROWS, ROWS), 0), iota((ROWS, ROWS), 1)
    allowed = (row16 % slots == col16 % slots) & (col16 // slots <= row16 // slots)
    fresh_bias = jnp.where(allowed, 0.0, -1e30)
    fresh_ref[...] = fresh.reshape(2, ROWS, -1)
    group = (acols * n) // (kv_heads * HD)
    per_block = acols // HD
    scale = 1.0 / math.sqrt(HD)
    contract = (((1,), (1,)), ((), ()))

    def attend_head(h):
        lanes = pl.ds(pl.multiple_of(h * HD, HD), HD)
        q = jnp.concatenate(
            [
                query[:, pl.ds(pl.multiple_of((h * group + g) * HD, HD), HD)]
                for g in range(group)
            ],
            axis=0,
        )
        old = lax.dot_general(q, kv[0, :, lanes], contract, preferred_element_type=f32)
        new = lax.dot_general(
            q, fresh_ref[0, :, lanes], contract, preferred_element_type=f32
        )
        old = old.reshape(group, ROWS, -1) * scale + bias[...][None]
        new = new.reshape(group, ROWS, -1) * scale + fresh_bias[None]
        top = jnp.maximum(
            jnp.max(old, axis=-1, keepdims=True), jnp.max(new, axis=-1, keepdims=True)
        )
        old = jnp.exp(old - top)
        new = jnp.exp(new - top)
        norm = jnp.sum(old, axis=-1, keepdims=True) + jnp.sum(new, axis=-1, keepdims=True)
        old = old.astype(bf16).reshape(group * ROWS, -1)
        new = new.astype(bf16).reshape(group * ROWS, -1)
        out = jnp.dot(old, kv[1, :, lanes], preferred_element_type=f32)
        out = out + jnp.dot(new, fresh_ref[1, :, lanes], preferred_element_type=f32)
        out = (out.reshape(group, ROWS, HD) / norm).astype(bf16)
        for g in range(group):
            place = g % per_block
            att_send[h * (group // per_block) + g // per_block, :, place * HD : (place + 1) * HD] = out[g]

    early = kv_heads // 2
    pl.loop(0, early)(attend_head)

    here = pl.ds(pl.multiple_of(me * cols, cols), cols)
    w2, w3 = taps[2:3, here], taps[3:4, here]
    tok4 = tok.reshape(n, 2, 8, cols)
    req_wait(pre_send, pre_recv, pre_ss, pre_rs)
    req_start(tok_send, tok_recv, tok_ss, tok_rs)
    pre4 = pre_recv[...].astype(f32).reshape(n, 2, 8, cols)
    first = pre4[:, 0] + tok4[:, 0] * w3[None]
    second = pre4[:, 1] + tok4[:, 0] * w2[None] + tok4[:, 1] * w3[None]
    mixed = jnp.stack([jax.nn.silu(first), jax.nn.silu(second)], axis=1)
    mixed = mixed.reshape(rows, cols).astype(bf16)
    loads[7].wait()
    part = lax.dot_general(mixed, pw[...], contract, preferred_element_type=f32)
    half = DT_RANK // 2
    maps = part[:, DT_RANK:]
    upper = maps.astype(bf16).astype(f32)
    maps = jnp.concatenate(
        [upper, maps - upper, jnp.zeros((rows, 128 - 4 * STATE), f32)], axis=1
    )
    for c in range(2):
        part_send[c * n : (c + 1) * n, :, :half] = (
            part[:, c * half : (c + 1) * half].astype(bf16).reshape(n, ROWS, half)
        )
        part_send[c * n : (c + 1) * n, :, half:] = maps.astype(bf16).reshape(n, ROWS, 128)

    @pl.loop(1, total)
    def _(k):
        peer = lax.rem(flat + k, total)
        all_copy(part_send.at[peer], part_recv, part_ss, part_rs, peer, flat).start()

    part_recv[pl.ds(flat, 1)] = part_send[pl.ds(flat, 1)]
    pl.loop(early, kv_heads)(attend_head)

    @pl.loop(1, total)
    def _(k):
        peer = lax.rem(flat + k, total)
        all_copy(part_send.at[peer], part_recv, part_ss, part_rs, peer, peer).wait_recv()

    summed = jnp.sum(part_recv[...].astype(f32), axis=0)
    low_send[...] = summed[:, :half].astype(bf16)

    @pl.loop(1, total)
    def _(k):
        peer = lax.rem(flat + k, total)
        all_copy(low_send, low_recv, low_ss, low_rs, peer, flat).start()

    low_recv[pl.ds(flat, 1)] = low_send[...][None]
    req_start(att_send, att_recv, att_ss, att_rs)
    att_recv[pl.ds(me, 1)] = att_send[pl.ds(me, 1)]
    square = jnp.concatenate(
        [summed[:, half:], jnp.zeros((128 - ROWS, 128), f32)], axis=0
    )
    flipped = jnp.transpose(square)
    maps_t[...] = flipped[: 2 * STATE] + flipped[2 * STATE : 4 * STATE]
    loads[8].wait()
    loads[9].wait()

    @pl.loop(1, total)
    def _(k):
        peer = lax.rem(flat + k, total)
        all_copy(low_send, low_recv, low_ss, low_rs, peer, peer).wait_recv()

    z = jnp.dot(low_recv[:n].reshape(rows, half), dtw[:half], preferred_element_type=f32)
    z = z + jnp.dot(low_recv[n:].reshape(rows, half), dtw[half:], preferred_element_type=f32)
    zbuf[...] = (z + dt_bias[:, here]).reshape(n, ROWS, cols)

    @pl.loop(0, n)
    def _(k):
        peer = lax.rem(me + 1 + k, n)
        block = zbuf[pl.ds(peer, 1)]
        delta = jnp.maximum(block, 0.0) + jnp.log1p(jnp.exp(-jnp.abs(block)))
        del_send[pl.ds(peer, 1)] = delta.astype(bf16)

        @pl.when(k < n - 1)
        def _():
            req_copy(del_send, del_recv, del_ss, del_rs, peer, me).start()

    del_recv[pl.ds(me, 1)] = del_send[pl.ds(me, 1)]
    for load in loads[10:13]:
        load.wait()
    req_wait(tok_send, tok_recv, tok_ss, tok_rs)

    @pl.loop(0, n)
    def _(k):
        peer = lax.rem(me - k + n, n)

        @pl.when(k > 0)
        def _():
            req_copy(del_send, del_recv, del_ss, del_rs, peer, peer).wait_recv()

        block = pl.ds(pl.multiple_of(peer * cols, cols), cols)
        delta = del_recv[peer].astype(f32)
        toks = tok_recv[peer].astype(f32)
        w2 = taps[2:3, block]
        w3 = taps[3:4, block]
        skip = skip_gain[:, block]
        x0 = pre[0:8, block] + toks[0:8] * w3
        x1 = pre[8:16, block] + toks[0:8] * w2 + toks[8:16] * w3
        x = jnp.concatenate([jax.nn.silu(x0), jax.nn.silu(x1)], axis=0)
        x = x.astype(bf16).astype(f32)
        dx = delta * x
        rate = -jnp.exp(decay[:, block])
        for s in range(slots):
            h = state[s, :, block]
            for t in range(STEPS):
                i = t * slots + s
                h = jnp.exp(delta[i : i + 1] * rate) * h + dx[i : i + 1] * maps_t[:STATE, i : i + 1]
                vbuf[i : i + 1, :] = jnp.sum(
                    h * maps_t[STATE:, i : i + 1], axis=0, keepdims=True
                )
        val_send[peer] = (vbuf[...] + skip * x).astype(bf16)

        @pl.when(k > 0)
        def _():
            req_copy(val_send, val_recv, val_ss, val_rs, peer, me).start()

    val_recv[pl.ds(me, 1)] = val_send[pl.ds(me, 1)]

    loads[13].wait()
    gate = jax.nn.silu(gate_in[...].reshape(rows, cols).astype(f32))
    req_wait(att_send, att_recv, att_ss, att_rs)
    att = jnp.dot(back, att_recv[...].reshape(rows, acols), preferred_element_type=f32)
    att_ref[...] = att.astype(bf16).reshape(att_ref.shape)
    req_wait(val_send, val_recv, val_ss, val_rs)
    val = jnp.dot(back, val_recv[...].reshape(rows, cols), preferred_element_type=f32)
    mamba_ref[...] = (val * gate).astype(bf16).reshape(mamba_ref.shape)

    req_drain(pre_send, pre_recv, pre_ss, pre_rs)
    req_drain(tok_send, tok_recv, tok_ss, tok_rs)
    req_drain(att_send, att_recv, att_ss, att_rs)
    req_drain(del_send, del_recv, del_ss, del_rs)
    req_drain(val_send, val_recv, val_ss, val_rs)

    @pl.loop(1, total)
    def _(k):
        peer = lax.rem(flat + k, total)
        all_copy(part_send.at[peer], part_recv, part_ss, part_rs, peer, flat).wait_send()
        all_copy(low_send, low_recv, low_ss, low_rs, peer, flat).wait_send()


def local_kernel(
    ssm_state,
    conv_state,
    token_input,
    gate_input,
    conv_weight,
    conv_bias,
    proj_weight,
    dt_weight,
    dt_bias,
    decay_log,
    skip_gain,
    queries,
    kv_pages,
    new_kv,
    page_table,
    context_len,
    decode_row,
):
    n = lax.axis_size("req")
    slots = ssm_state.shape[0]
    width = ssm_state.shape[2]
    total = decode_row.shape[0]
    cols = token_input.shape[2]
    acols = queries.shape[2] // n
    kv_heads = KVH // lax.axis_size("tp")
    pages, page = kv_pages.shape[1:3]
    rows = total * STEPS
    kv = kv_pages.reshape(2, pages * page, -1)
    half = DT_RANK // 2
    bf16, f32 = jnp.bfloat16, jnp.float32
    vmem = pl.BlockSpec(memory_space=pltpu.VMEM)
    hbm = pl.BlockSpec(memory_space=pl.ANY)
    dma = pltpu.SemaphoreType.DMA
    mamba, attended = pl.pallas_call(
        functools.partial(block_kernel, n, slots, cols, acols, kv_heads),
        out_shape=(
            jax.ShapeDtypeStruct((total, STEPS, cols), bf16),
            jax.ShapeDtypeStruct((total, STEPS, acols), bf16),
        ),
        in_specs=[hbm] * 14 + [vmem] * 3,
        out_specs=(vmem, vmem),
        scratch_shapes=[
            pltpu.VMEM(kv.shape, bf16),
            pltpu.VMEM(queries.shape, bf16),
            pltpu.VMEM(new_kv.shape, bf16),
            pltpu.VMEM(proj_weight.shape[::-1], bf16),
            pltpu.VMEM(dt_weight.shape, bf16),
            pltpu.VMEM(ssm_state.shape, f32),
            pltpu.VMEM(decay_log.shape, f32),
            pltpu.VMEM(gate_input.shape, bf16),
            pltpu.VMEM((1, width), f32),
            pltpu.VMEM((1, width), f32),
            pltpu.VMEM((CONV - 1, slots, width), f32),
            pltpu.VMEM(conv_weight.shape, f32),
            pltpu.VMEM((1, width), f32),
            pltpu.VMEM(token_input.shape, bf16),
            pltpu.VMEM((ROWS, width), f32),
            pltpu.VMEM((ROWS, pages * page), f32),
            pltpu.VMEM((ROWS, queries.shape[2]), bf16),
            pltpu.VMEM((2, ROWS, new_kv.shape[3]), bf16),
            pltpu.VMEM((n, ROWS, cols), bf16),
            pltpu.VMEM((n, ROWS, cols), bf16),
            pltpu.VMEM((n, ROWS, cols), bf16),
            pltpu.VMEM((n, ROWS, cols), bf16),
            pltpu.VMEM((2 * n, ROWS, half + 128), bf16),
            pltpu.VMEM((2 * n, ROWS, half + 128), bf16),
            pltpu.VMEM((ROWS, half), bf16),
            pltpu.VMEM((2 * n, ROWS, half), bf16),
            pltpu.VMEM((n, ROWS, cols), bf16),
            pltpu.VMEM((n, ROWS, cols), bf16),
            pltpu.VMEM((n, ROWS, cols), bf16),
            pltpu.VMEM((n, ROWS, cols), bf16),
            pltpu.VMEM((n, ROWS, acols), bf16),
            pltpu.VMEM((n, ROWS, acols), bf16),
            pltpu.VMEM((n, ROWS, cols), f32),
            pltpu.VMEM((ROWS, cols), f32),
            pltpu.VMEM((2 * STATE, 128), f32),
            dma((14,)),
            dma((n,)),
            dma((n,)),
            dma((n,)),
            dma((n,)),
            dma((2 * n,)),
            dma((2 * n,)),
            dma((2 * n,)),
            dma((2 * n,)),
            dma((n,)),
            dma((n,)),
            dma((n,)),
            dma((n,)),
            dma((n,)),
            dma((n,)),
        ],
        compiler_params=pltpu.CompilerParams(
            collective_id=0, has_side_effects=True, vmem_limit_bytes=60 * 2**20
        ),
    )(
        kv,
        queries,
        new_kv,
        proj_weight.T,
        dt_weight,
        ssm_state,
        decay_log,
        gate_input,
        dt_bias[None],
        skip_gain[None],
        conv_state.transpose(1, 0, 2),
        conv_weight,
        conv_bias[None],
        token_input,
        decode_row[None],
        page_table,
        context_len[None],
    )
    return mamba, attended


def solution(mesh):
    in_specs = (
        P(("groups", "req"), None, "tp"),
        P(("groups", "req"), None, "tp"),
        P("groups", None, ("tp", "req")),
        P("groups", None, ("tp", "req")),
        P(None, "tp"),
        P("tp"),
        P(("tp", "req"), None),
        P(None, ("tp", "req")),
        P("tp"),
        P(None, "tp"),
        P("tp"),
        P(("groups", "req"), None, "tp"),
        P(None, ("groups", "req"), None, "tp"),
        P(("groups", "req"), None, None, "tp"),
        P(("groups", "req"), None),
        P(("groups", "req")),
        P("groups"),
    )
    out_specs = (P("groups", None, ("tp", "req")), P("groups", None, ("tp", "req")))
    kernel_fits = mesh.shape["req"] <= 8 and mesh.shape["tp"] == 2
    body = local_kernel if kernel_fits else local
    return jax.shard_map(body, mesh=mesh, in_specs=in_specs, out_specs=out_specs, check_vma=False)
```
